256 devices in a mesh: blk: 64 (over x, y_hi, z), rep: 4 (over y_lo, core).
Axes of the slice: x: 4, y: 4 (y_hi: 2, y_lo: 2; y = y_hi * 2 + y_lo), z: 8, core: 2. Of those that a mesh axis runs over, the one named last changes fastest.
Arguments:
- features: bfloat16 [32768, 512], P('blk', 'rep'), may hold values from -6 to 6
- row_target: int32 [32768], P('blk'), may hold values from 0 to 32767, as said below
- tile_values: bfloat16 [64, 64, 4, 128, 128], P('blk'), may hold values from -0.25 to 0.25
- tile_rows: int32 [64, 64, 4], P('blk'), may hold values from 0 to 3, as said below
- tile_cols: int32 [64, 64, 4], P('blk'), may hold values from 0 to 3, as said below
- tile_counts: int32 [64, 64], P('blk'), may hold values from 0 to 4, as said below
- weight: bfloat16 [512, 512], P('rep'), may hold values from -0.25 to 0.25
- layer_bias: float32 [512], replicated, may hold values from -3 to 3
- out_grad: bfloat16 [32768, 512], P('blk'), may hold values from -0.75 to 0.75
Outputs:
- output: bfloat16 [32768, 512], P(('blk', 'rep'))
- weight_grad: float32 [512, 512], P('rep')
- bias_grad: float32 [512], replicated
- feature_grad: bfloat16 [32768, 512], P('blk', 'rep')
The draws below stay inside these ranges and needn't reach their ends.
Inputs may be any that keep to these rules, and one draw needn't show every extreme that they name: `row_target`: a permutation of the 32768 rows; the rows of one loader block of 512 rows bound for one partition number at most 16, and this many in every draw. `tile_rows`: within one pair of partitions the live slots name distinct tile positions. `tile_cols`: within one pair of partitions the live slots name distinct tile positions. `tile_counts`: every pair of a partition with itself has all 4 slots live; each row partition has live slots with exactly 6 other partitions, and none with the rest.
All inputs are finite; a program needn't handle non-finite values.
Results may differ from the reference program's by a relative error of at most 0.0061.
Values may be sent and summed in bfloat16 or wider, within the bound.
A program may use at most 128 MiB of HBM per device.

```python
import jax
import jax.numpy as jnp
from jax import lax

F = 512
TILE = 128
SLOTS = 4
PARTNERS = 6
ROWS = 512
NODES = 32768
REACH = 608
N_BLK = 64


def draw_row_target(key, part):
    baseline = ROWS // N_BLK
    quarter = N_BLK // 4
    first_key, second_key, third_key = jax.random.split(key, 3)
    offsets_order = jax.random.permutation(first_key, N_BLK)
    loads = jnp.full((N_BLK,), baseline, jnp.int32)
    loads = loads.at[offsets_order[:quarter]].set(2 * baseline)
    loads = loads.at[offsets_order[quarter:2 * quarter]].set(0)
    sources = jnp.arange(N_BLK, dtype=jnp.int32)
    counts = loads[(sources[None, :] - sources[:, None]) % N_BLK]
    arrival = jnp.cumsum(counts, axis=0) - counts
    starting = jnp.cumsum(counts, axis=1) - counts
    inner = jax.vmap(lambda single: jax.random.permutation(single, ROWS).astype(jnp.int32))(jax.random.split(second_key, N_BLK))
    shuffle = jax.vmap(lambda single: jax.random.permutation(single, ROWS).astype(jnp.int32))(jax.random.split(third_key, N_BLK))
    positions = jnp.arange(ROWS, dtype=jnp.int32)

    def one_source(source, count_row, start_row, order_row):
        target = jnp.repeat(sources, count_row, total_repeat_length=ROWS)
        ranked = positions - start_row[target]
        landing = arrival[source, target] + ranked
        value = target * ROWS + inner[target, landing]
        return (source * ROWS + order_row, value)
    where_from, value = jax.vmap(one_source)(sources, counts, starting, shuffle)
    return jnp.zeros((N_BLK * ROWS,), jnp.int32).at[where_from.reshape(-1)].set(value.reshape(-1))


def tile_places(key):
    folded = jax.random.fold_in(key, 11)
    row_tiles = ROWS // TILE
    keys = jax.random.split(folded, N_BLK * N_BLK)
    picks = jax.vmap(lambda single: jax.random.permutation(single, row_tiles * row_tiles)[:SLOTS])(keys)
    return (picks.reshape(N_BLK, N_BLK, SLOTS).astype(jnp.int32), row_tiles)


def draw_tile_rows(key, part):
    picks, row_tiles = tile_places(key)
    return picks // row_tiles


def draw_tile_cols(key, part):
    picks, row_tiles = tile_places(key)
    return picks % row_tiles


def draw_tile_counts(key, part):
    first_key, second_key = jax.random.split(key, 2)
    row_keys = jax.random.split(first_key, N_BLK)
    offsets = jax.vmap(lambda single: jax.random.permutation(single, N_BLK - 1)[:PARTNERS].astype(jnp.int32))(row_keys)
    diagonal = jnp.arange(N_BLK, dtype=jnp.int32)
    partner_cols = (diagonal[:, None] + 1 + offsets) % N_BLK
    levels = jax.random.randint(second_key, (N_BLK, PARTNERS), 1, SLOTS + 1).astype(jnp.int32)
    counts = jnp.zeros((N_BLK, N_BLK), jnp.int32)
    counts = counts.at[diagonal[:, None], partner_cols].set(levels)
    counts = counts.at[diagonal, diagonal].set(SLOTS)
    return counts.astype(jnp.int32)


def shard_levels(key, shape, cuts, low, high):
    loudness, own = 1.0, jax.random.fold_in(key, 6)
    for dim, parts in cuts:
        steps = jnp.exp(jax.random.uniform(jax.random.fold_in(own, dim), (parts,), jnp.float32, low / len(cuts), high / len(cuts)))
        loudness = loudness * jnp.repeat(steps, shape[dim] // parts).reshape([-1 if axis == dim else 1 for axis in range(len(shape))])
    return loudness


def noise(own_key, extent, deviation, bound, cuts=(), kind=jnp.bfloat16):
    loudness = shard_levels(own_key, extent, cuts, -0.22, 0.18) if cuts else 1.0
    array = jax.random.normal(own_key, extent, jnp.float32) * deviation * loudness
    return jnp.minimum(jnp.maximum(array, -bound), bound).astype(kind)


def setup_inputs(seed: int = 0) -> dict:
    splits = jax.random.split(jax.random.key(seed), 10)
    features = noise(splits[0], (NODES, F), 1.0, 6.0, ((0, 64), (1, 4)))
    row_target = draw_row_target(jax.random.fold_in(splits[9], 71), 0)
    tile_values = noise(splits[2], (N_BLK, N_BLK, SLOTS, TILE, TILE), REACH ** -0.5, 0.25, ((0, 64),))
    tile_rows = draw_tile_rows(jax.random.fold_in(splits[9], 71), 0)
    tile_cols = draw_tile_cols(jax.random.fold_in(splits[9], 71), 0)
    tile_counts = draw_tile_counts(jax.random.fold_in(splits[9], 71), 0)
    weight = noise(splits[6], (F, F), F ** -0.5, 0.25, ((0, 4),))
    layer_bias = noise(splits[7], (F,), 0.5, 3.0, (), jnp.float32)
    out_grad = noise(splits[8], (NODES, F), 0.125, 0.75, ((0, 64),))
    return dict(features=features, row_target=row_target, tile_values=tile_values, tile_rows=tile_rows, tile_cols=tile_cols, tile_counts=tile_counts, weight=weight, layer_bias=layer_bias, out_grad=out_grad)


def reference(features, row_target, tile_values, tile_rows, tile_cols, tile_counts, weight, layer_bias, out_grad):
    row_tiles = ROWS // TILE
    node_count = features.shape[0]
    regrouped = jnp.zeros_like(features).at[row_target].set(features)
    reg_tiles = regrouped.astype(jnp.float32).reshape(node_count // TILE, TILE, F)
    slot_ids = jnp.arange(SLOTS, dtype=jnp.int32)
    blocks = jnp.arange(N_BLK, dtype=jnp.int32)
    tile_ids = jnp.arange(row_tiles, dtype=jnp.int32)

    def row_part(part):
        values = tile_values[part].astype(jnp.float32)
        live = slot_ids[None, :] < tile_counts[part][:, None]
        column = blocks[:, None] * row_tiles + tile_cols[part]
        inputs = reg_tiles[column]
        product = jnp.einsum("qsij,qsjf->qsif", values, inputs, precision=lax.Precision.HIGHEST)
        place = ((tile_rows[part][..., None] == tile_ids) & live[..., None]).astype(jnp.float32)
        return jnp.einsum("qsr,qsif->rif", place, product, precision=lax.Precision.HIGHEST).reshape(ROWS, F)

    mixed = lax.map(row_part, blocks).reshape(node_count, F).astype(jnp.bfloat16)
    pre = jnp.dot(mixed, weight, preferred_element_type=jnp.float32) + layer_bias
    sigma = jax.nn.sigmoid(pre)
    output = (pre * sigma).astype(jnp.bfloat16)
    pre_grad = (out_grad.astype(jnp.float32) * sigma * (1.0 + pre * (1.0 - sigma))).astype(jnp.bfloat16)
    bias_grad = jnp.sum(pre_grad.astype(jnp.float32), axis=0)
    weight_grad = jnp.dot(mixed.T, pre_grad, preferred_element_type=jnp.float32)
    mixed_grad = jnp.dot(pre_grad, weight.T, preferred_element_type=jnp.float32).astype(jnp.bfloat16)
    grad_tiles = mixed_grad.astype(jnp.float32).reshape(node_count // TILE, TILE, F)

    def col_part(part):
        values = tile_values[:, part].astype(jnp.float32)
        live = slot_ids[None, :] < tile_counts[:, part][:, None]
        source = blocks[:, None] * row_tiles + tile_rows[:, part]
        inputs = grad_tiles[source]
        product = jnp.einsum("psij,psif->psjf", values, inputs, precision=lax.Precision.HIGHEST)
        place = ((tile_cols[:, part][..., None] == tile_ids) & live[..., None]).astype(jnp.float32)
        return jnp.einsum("psr,psjf->rjf", place, product, precision=lax.Precision.HIGHEST).reshape(ROWS, F)

    feature_grad = lax.map(col_part, blocks).reshape(node_count, F).astype(jnp.bfloat16)
    return output, weight_grad, bias_grad, feature_grad
```

```python
import jax
import jax.numpy as jnp
from jax import lax
from jax.sharding import PartitionSpec as P

PARTNERS = 6
BF = jnp.bfloat16
F32 = jnp.float32


def one_hot(condition):
    return condition.astype(BF)


def dot(a, b, dims=((1,), (0,))):
    return lax.dot_general(a, b, (dims, ((), ())), preferred_element_type=F32)


def exchange(x):
    return lax.all_to_all(x, "blk", split_axis=0, concat_axis=0, tiled=True)


def per_device(
    features,
    row_target,
    tile_values,
    tile_rows,
    tile_cols,
    tile_counts,
    weight,
    layer_bias,
    out_grad,
):
    blocks = lax.axis_size("blk")
    members = lax.axis_size("rep")
    me = lax.axis_index("blk")
    member = lax.axis_index("rep")
    rows, cols = features.shape
    slots, tile = tile_values.shape[2:4]
    tiles = rows // tile
    bucket = 2 * rows // blocks
    piece = rows // blocks

    full_weight = lax.all_gather(weight, "rep", axis=0, tiled=True)
    all_counts = lax.all_gather(tile_counts[0], "blk", axis=0).reshape(blocks, blocks)

    ids = jnp.arange(blocks, dtype=jnp.int32)
    target = row_target // rows
    landing = row_target % rows
    hits = target[None, :] == ids[:, None]
    at = jnp.arange(rows, dtype=jnp.int32)
    earlier = dot(one_hot(hits), one_hot(at[:, None] < at[None, :]))
    rank = jnp.sum(jnp.where(hits, earlier, 0.0), axis=0).astype(jnp.int32)
    slot = target * bucket + rank
    to_slot = slot[None, :] == jnp.arange(blocks * bucket, dtype=jnp.int32)[:, None]
    send_rows = dot(one_hot(to_slot), features).astype(BF)
    send_where = jnp.sum(jnp.where(to_slot, landing[None, :] + 1, 0), axis=1) - 1
    got_rows = exchange(send_rows.reshape(blocks, bucket, cols)).reshape(-1, cols)
    got_where = exchange(send_where.reshape(blocks, bucket)).reshape(-1)
    regrouped = dot(one_hot(got_where[None, :] == at[:, None]), got_rows).astype(BF)

    partner = (all_counts > 0) & (ids[:, None] != ids[None, :])
    order = dot(one_hot(partner), one_hot(ids[:, None] < ids[None, :]))
    wanted = jnp.arange(PARTNERS, dtype=F32)
    choose = partner[:, None, :] & (order[:, None, :] == wanted[None, :, None])
    flat_choose = one_hot(choose).reshape(blocks * PARTNERS, blocks)
    mine = lax.dynamic_index_in_dim(choose, me, 0, keepdims=False)
    mine = jnp.concatenate([mine, (ids == me)[None]], axis=0).astype(jnp.int32)
    which = jnp.sum(mine * ids[None, :], axis=1)
    meets = PARTNERS + 1

    row_of = jnp.sum(mine[:, :, None] * tile_rows[0][None], axis=1)
    col_of = jnp.sum(mine[:, :, None] * tile_cols[0][None], axis=1)
    live = jnp.sum(mine * tile_counts[0][None], axis=1)
    live = jnp.arange(slots, dtype=jnp.int32)[None, :] < live[:, None]
    tile_ids = jnp.arange(tiles, dtype=jnp.int32)
    spot = (
        live[:, :, None, None]
        & (row_of[:, :, None, None] == tile_ids[None, None, :, None])
        & (col_of[:, :, None, None] == tile_ids[None, None, None, :])
    )
    adjacency = []
    for k in range(meets):
        values = lax.dynamic_index_in_dim(tile_values[0], which[k], 0, keepdims=False)
        dense = jnp.zeros((tiles, tile, tiles, tile), BF)
        for s in range(slots):
            dense = jnp.where(
                spot[k, s][:, None, :, None], values[s][None, :, None, :], dense
            )
        adjacency.append(dense.reshape(rows, rows))
    adjacency = jnp.concatenate(adjacency, axis=1)

    spread = exchange(regrouped.reshape(blocks, piece, cols)).reshape(blocks, piece * cols)
    served = dot(flat_choose, spread).astype(BF)
    served = exchange(served.reshape(blocks, PARTNERS * piece, cols))
    served = served.reshape(blocks, PARTNERS, piece, cols).transpose(1, 0, 2, 3)
    inputs = jnp.concatenate([served.reshape(PARTNERS * rows, cols), regrouped], axis=0)
    mixed = dot(adjacency, inputs).astype(BF)

    full_mixed = lax.all_gather(mixed, "rep", axis=1, tiled=True)
    pre = dot(full_mixed, full_weight) + layer_bias
    sigma = jax.nn.sigmoid(pre)
    share = rows // members
    output = lax.dynamic_slice_in_dim((pre * sigma).astype(BF), member * share, share, 0)
    pre_grad = (out_grad.astype(F32) * sigma * (1.0 + pre * (1.0 - sigma))).astype(BF)
    mixed_grad = dot(pre_grad, weight, ((1,), (1,))).astype(BF)

    terms = dot(adjacency, mixed_grad, ((0,), (0,)))
    own = terms[PARTNERS * rows :]
    away = terms[: PARTNERS * rows].astype(BF).reshape(PARTNERS, blocks, piece, cols)
    away = exchange(away.transpose(1, 0, 2, 3).reshape(blocks, PARTNERS * piece, cols))
    away = away.reshape(blocks * PARTNERS, piece * cols)
    summed = dot(flat_choose, away, ((0,), (0,)))
    back = exchange(summed.reshape(blocks, piece, cols)).reshape(rows, cols)
    feature_grad = (back + own).astype(BF)

    weight_part = dot(mixed, pre_grad, ((0,), (0,)))
    bias_part = jnp.sum(pre_grad.astype(F32), axis=0)
    bias_grad = jnp.sum(lax.all_gather(bias_part, "blk", axis=0), axis=0)
    wide = weight_part.shape[1]
    weight_part = exchange(weight_part.reshape(blocks, -1, wide))
    weight_grad = lax.all_gather(jnp.sum(weight_part, axis=0), "blk", axis=0, tiled=True)
    return (output, weight_grad, bias_grad, feature_grad)


def solution(mesh):
    in_specs = (
        P("blk", "rep"),
        P("blk"),
        P("blk", None, None, None, None),
        P("blk", None, None),
        P("blk", None, None),
        P("blk", None),
        P("rep", None),
        P(),
        P("blk", None),
    )
    out_specs = (P(("blk", "rep"), None), P("rep", None), P(), P("blk", "rep"))
    return jax.shard_map(
        per_device, mesh=mesh, in_specs=in_specs, out_specs=out_specs, check_vma=False
    )
```

```python
import jax
import jax.numpy as jnp
from jax import lax
from jax.sharding import PartitionSpec as P

PARTNERS = 6
BF = jnp.bfloat16
F32 = jnp.float32


def one_hot(condition):
    return condition.astype(BF)


def dot(a, b, dims=((1,), (0,))):
    return lax.dot_general(a, b, (dims, ((), ())), preferred_element_type=F32)


def exchange(x):
    return lax.all_to_all(x, "blk", split_axis=0, concat_axis=0, tiled=True)


def everywhere(x, blocks):
    return exchange(jnp.broadcast_to(x[None], (blocks, *x.shape)))


def per_device(
    features,
    row_target,
    tile_values,
    tile_rows,
    tile_cols,
    tile_counts,
    weight,
    layer_bias,
    out_grad,
):
    blocks = lax.axis_size("blk")
    members = lax.axis_size("rep")
    me = lax.axis_index("blk")
    member = lax.axis_index("rep")
    rows, cols = features.shape
    slots, tile = tile_values.shape[2:4]
    tiles = rows // tile
    bucket = 2 * rows // blocks
    piece = rows // blocks

    full_weight = lax.all_gather(weight, "rep", axis=0, tiled=True)
    all_counts = everywhere(tile_counts[0], blocks)

    ids = jnp.arange(blocks, dtype=jnp.int32)
    target = row_target // rows
    landing = row_target % rows
    hits = target[None, :] == ids[:, None]
    at = jnp.arange(rows, dtype=jnp.int32)
    earlier = dot(one_hot(hits), one_hot(at[:, None] < at[None, :]))
    rank = jnp.sum(jnp.where(hits, earlier, 0.0), axis=0).astype(jnp.int32)
    slot = target * bucket + rank
    to_slot = slot[None, :] == jnp.arange(blocks * bucket, dtype=jnp.int32)[:, None]
    send_rows = dot(one_hot(to_slot), features).astype(BF)
    send_where = jnp.sum(jnp.where(to_slot, landing[None, :] + 1, 0), axis=1) - 1
    got_rows = exchange(send_rows.reshape(blocks, bucket, cols)).reshape(-1, cols)
    got_where = exchange(send_where.reshape(blocks, bucket)).reshape(-1)
    regrouped = dot(one_hot(got_where[None, :] == at[:, None]), got_rows).astype(BF)

    partner = (all_counts > 0) & (ids[:, None] != ids[None, :])
    order = dot(one_hot(partner), one_hot(ids[:, None] < ids[None, :]))
    wanted = jnp.arange(PARTNERS, dtype=F32)
    choose = partner[:, None, :] & (order[:, None, :] == wanted[None, :, None])
    flat_choose = one_hot(choose).reshape(blocks * PARTNERS, blocks)
    mine = lax.dynamic_index_in_dim(choose, me, 0, keepdims=False)
    mine = jnp.concatenate([mine, (ids == me)[None]], axis=0).astype(jnp.int32)
    which = jnp.sum(mine * ids[None, :], axis=1)
    meets = PARTNERS + 1

    row_of = jnp.sum(mine[:, :, None] * tile_rows[0][None], axis=1)
    col_of = jnp.sum(mine[:, :, None] * tile_cols[0][None], axis=1)
    live = jnp.sum(mine * tile_counts[0][None], axis=1)
    live = jnp.arange(slots, dtype=jnp.int32)[None, :] < live[:, None]
    tile_ids = jnp.arange(tiles, dtype=jnp.int32)
    spot = (
        live[:, :, None, None]
        & (row_of[:, :, None, None] == tile_ids[None, None, :, None])
        & (col_of[:, :, None, None] == tile_ids[None, None, None, :])
    )
    adjacency = []
    for k in range(meets):
        values = lax.dynamic_index_in_dim(tile_values[0], which[k], 0, keepdims=False)
        dense = jnp.zeros((tiles, tile, tiles, tile), BF)
        for s in range(slots):
            dense = jnp.where(
                spot[k, s][:, None, :, None], values[s][None, :, None, :], dense
            )
        adjacency.append(dense.reshape(rows, rows))
    adjacency = jnp.concatenate(adjacency, axis=1)

    spread = exchange(regrouped.reshape(blocks, piece, cols)).reshape(blocks, piece * cols)
    served = dot(flat_choose, spread).astype(BF)
    served = exchange(served.reshape(blocks, PARTNERS * piece, cols))
    served = served.reshape(blocks, PARTNERS, piece, cols).transpose(1, 0, 2, 3)
    inputs = jnp.concatenate([served.reshape(PARTNERS * rows, cols), regrouped], axis=0)
    mixed = dot(adjacency, inputs).astype(BF)

    full_mixed = lax.all_gather(mixed, "rep", axis=1, tiled=True)
    pre = dot(full_mixed, full_weight) + layer_bias
    sigma = jax.nn.sigmoid(pre)
    share = rows // members
    output = lax.dynamic_slice_in_dim((pre * sigma).astype(BF), member * share, share, 0)
    pre_grad = (out_grad.astype(F32) * sigma * (1.0 + pre * (1.0 - sigma))).astype(BF)
    mixed_grad = dot(pre_grad, weight, ((1,), (1,))).astype(BF)

    terms = dot(adjacency, mixed_grad, ((0,), (0,)))
    own = terms[PARTNERS * rows :]
    away = terms[: PARTNERS * rows].astype(BF).reshape(PARTNERS, blocks, piece, cols)
    away = exchange(away.transpose(1, 0, 2, 3).reshape(blocks, PARTNERS * piece, cols))
    away = away.reshape(blocks * PARTNERS, piece * cols)
    summed = dot(flat_choose, away, ((0,), (0,)))
    back = exchange(summed.reshape(blocks, piece, cols)).reshape(rows, cols)
    feature_grad = (back + own).astype(BF)

    weight_part = dot(mixed, pre_grad, ((0,), (0,)))
    bias_part = jnp.sum(pre_grad.astype(F32), axis=0)
    wide = weight_part.shape[1]
    weight_part = exchange(weight_part.reshape(blocks, -1, wide))
    weight_sum = jnp.sum(weight_part, axis=0)
    bias_terms = everywhere(bias_part[None], blocks)
    weight_grad = everywhere(weight_sum, blocks).reshape(weight.shape)
    bias_grad = jnp.sum(bias_terms, axis=(0, 1))
    return (output, weight_grad, bias_grad, feature_grad)


def solution(mesh):
    in_specs = (
        P("blk", "rep"),
        P("blk"),
        P("blk", None, None, None, None),
        P("blk", None, None),
        P("blk", None, None),
        P("blk", None),
        P("rep", None),
        P(),
        P("blk", None),
    )
    out_specs = (P(("blk", "rep"), None), P("rep", None), P(), P("blk", "rep"))
    return jax.shard_map(
        per_device, mesh=mesh, in_specs=in_specs, out_specs=out_specs, check_vma=False
    )
```

```python
import functools
import math

import jax
import jax.numpy as jnp
from jax import lax
from jax.experimental import pallas as pl
from jax.experimental.pallas import tpu as pltpu
from jax.sharding import PartitionSpec as P

PARTNERS = 6
BF = jnp.bfloat16
F32 = jnp.float32
MESH = pl.DeviceIdType.MESH
LANES = 128
UNIT = 8


def dot(a, b, dims=((1,), (0,))):
    return lax.dot_general(a, b, (dims, ((), ())), preferred_element_type=F32)


def iota(shape, dim):
    return lax.broadcasted_iota(jnp.int32, shape, dim).astype(F32)


def split(x, by):
    whole = jnp.floor((x + 0.5) * (1.0 / by))
    return whole, x - whole * by


def as_rows(ref):
    return ref.reshape(math.prod(ref.shape[:-1]), ref.shape[-1])


def get_rows(ref):
    return as_rows(ref)[...]


def put_rows(ref, value):
    as_rows(ref)[...] = value


def ones_where(condition):
    return jnp.where(condition, 1.0, 0.0).astype(BF)


def kernel(
    blocks,
    members,
    feat,
    target_ref,
    pos,
    tile_hbm,
    w_ref,
    bias_ref,
    og_ref,
    out_ref,
    wg_ref,
    bg_ref,
    fg_ref,
    tv,
    load_s,
    load_r,
    spread_s,
    spread_r,
    pick_t,
    pick,
    serve_s,
    serve_r,
    adj,
    adj_t,
    mixed_r,
    w_all,
    pg,
    outs,
    mg,
    own,
    term_s,
    term_r,
    sum_s,
    sum_r,
    grad_s,
    grad_r,
    total_s,
    total_r,
    find,
    send_sem,
    recv_sem,
    tile_sem,
):
    me = lax.axis_index("blk")
    member = lax.axis_index("rep")
    rows, cols = feat.shape
    slots, tile = tv.shape[1:3]
    tiles = rows // tile
    bucket = 2 * rows // blocks
    wide = w_ref.shape[1]
    unit_rows = bucket + UNIT
    loaded = blocks * unit_rows
    served = blocks * PARTNERS * UNIT
    meets = PARTNERS + 1

    load_tiles = pltpu.make_async_copy(tile_hbm, tv, tile_sem)
    load_tiles.start()
    barrier = pltpu.get_barrier_semaphore()

    def greet(d, _):
        pl.semaphore_signal(
            barrier, inc=1, device_id=(lax.rem(me + d, blocks), member), device_id_type=MESH
        )
        return 0

    lax.fori_loop(1, blocks, greet, 0)
    for d in range(1, members):
        pl.semaphore_signal(
            barrier, inc=1, device_id=(me, lax.rem(member + d, members)), device_id_type=MESH
        )

    def send_all(phase, source, dest):
        def one(d, _):
            peer = lax.rem(me + d, blocks)
            pltpu.make_async_remote_copy(
                src_ref=source(peer),
                dst_ref=dest,
                send_sem=send_sem.at[phase],
                recv_sem=recv_sem.at[phase],
                device_id=(peer, member),
                device_id_type=MESH,
            ).start()
            return 0

        lax.fori_loop(1, blocks, one, 0)

    def send_members(phase, source, dest):
        for d in range(1, members):
            pltpu.make_async_remote_copy(
                src_ref=source,
                dst_ref=dest,
                send_sem=send_sem.at[phase],
                recv_sem=recv_sem.at[phase],
                device_id=(me, lax.rem(member + d, members)),
                device_id_type=MESH,
            ).start()

    def bytes_of(phase, ref):
        return pltpu.make_async_remote_copy(
            src_ref=ref,
            dst_ref=ref,
            send_sem=send_sem.at[phase],
            recv_sem=recv_sem.at[phase],
            device_id=(me, member),
            device_id_type=MESH,
        )

    def others(ref):
        return ref.at[pl.ds(0, ref.shape[0] - 1)]

    def scan(q, state):
        count, found = state
        live = (pos[0, q] >= 0) & (q != me)
        found = tuple(
            jnp.where(live & (count == k), q, f) for k, f in enumerate(found)
        )
        return count + jnp.where(live, 1, 0), found

    zero = jnp.int32(0)
    _, partners = lax.fori_loop(0, blocks, scan, (zero, (zero,) * PARTNERS))

    target = target_ref[...]
    goal, landing = split(target.astype(F32), rows)
    hits = ones_where(goal == iota((blocks, rows), 0))
    before = ones_where(iota((rows, rows), 0) < iota((rows, rows), 1))
    earlier = dot(hits, before)
    rank = jnp.sum(hits.astype(F32) * earlier, axis=0, keepdims=True)
    high, low = split(landing + 1.0, 16)
    of_rank = ones_where(rank == iota((LANES, rows), 0))
    on_lanes = ((1,), (1,))
    land_high = dot(hits * high.astype(BF), of_rank, on_lanes)
    land_low = dot(hits * low.astype(BF), of_rank, on_lanes)
    lane = lax.broadcasted_iota(jnp.int32, (blocks, LANES), 1)
    listed = jnp.zeros((blocks, LANES), jnp.int32)
    for k in range(PARTNERS):
        listed = jnp.where(lane == k, partners[k], listed)
    notes = jnp.concatenate([land_high, land_low, listed.astype(F32)], axis=0).astype(BF)
    to_unit = ones_where(goal * unit_rows + rank == iota((loaded, rows), 0))
    n_notes = 3 * blocks
    unit, inside = split(iota((loaded, n_notes), 0), unit_rows)
    kind, whose = split(iota((loaded, n_notes), 1), blocks)
    to_note = ones_where((unit == whose) & (inside == kind + bucket))
    filled = dot(to_unit, feat[...]) + dot(to_note, notes)
    put_rows(load_s, filled.astype(BF))

    pl.semaphore_wait(barrier, blocks + members - 2)
    send_all(0, lambda p: load_s.at[p], load_r.at[me])
    send_members(7, w_ref, w_all.at[member])
    load_r[me] = load_s[me]
    w_all[member] = w_ref[...]
    unit, inside = split(iota((n_notes, loaded), 1), unit_rows)
    kind, whose = split(iota((n_notes, loaded), 0), blocks)
    find[...] = ones_where((unit == whose) & (inside == kind + bucket))
    bytes_of(0, others(load_r)).wait_recv()

    got = get_rows(load_r)
    notes = dot(find[...], got)
    unit, inside = split(iota((blocks, loaded), 1), unit_rows)
    fold = ones_where(iota((LANES, loaded), 0) == split(iota((LANES, loaded), 1), unit_rows)[1])
    lands = 16.0 * dot(notes[:blocks].astype(BF), fold) + dot(
        notes[blocks : 2 * blocks].astype(BF), fold
    )
    lands = jnp.where(unit == iota((blocks, loaded), 0), lands, 0.0)
    lands = jnp.sum(lands, axis=0, keepdims=True) - 1.0
    regroup = ones_where(lands == iota((rows, loaded), 0))
    regrouped = dot(regroup, got).astype(BF)
    put_rows(spread_s, regrouped)
    send_all(1, lambda p: spread_s.at[p], spread_r.at[me])
    spread_r[me] = spread_s[me]

    lists = notes[2 * blocks :].astype(BF)
    chunk = rows

    def fill_pick_t(i, _):
        at = iota((chunk, blocks), 0) + (i * chunk).astype(F32)
        for_whom = ones_where(split(at, PARTNERS * UNIT)[0] == iota((chunk, blocks), 1))
        lane_at = iota((chunk, LANES), 0) + (i * chunk).astype(F32)
        nth, row = split(lane_at, UNIT)
        nth = split(nth, PARTNERS)[1]
        listed = jnp.where(nth == iota((chunk, LANES), 1), dot(for_whom, lists), 0.0)
        wanted = dot(listed.astype(BF), jnp.ones((LANES, rows), BF))
        row = iota((chunk, rows), 0) + (i * chunk).astype(F32)
        row = split(row, UNIT)[1]
        match = ones_where(wanted * UNIT + row == iota((chunk, rows), 1))
        pick_t[pl.ds(pl.multiple_of(i * chunk, chunk), chunk), :] = match
        return 0

    lax.fori_loop(0, served // chunk, fill_pick_t, 0)
    bytes_of(1, others(spread_r)).wait_recv()
    serving = dot(pick_t[...], get_rows(spread_r)).astype(BF)
    put_rows(serve_s, serving)
    send_all(2, lambda p: serve_s.at[p], serve_r.at[:, me])
    serve_r[:, me] = serve_s[me]

    load_tiles.wait()
    for k in range(meets):
        q = me if k == PARTNERS else partners[k]
        places = [pos[s, q] for s in range(slots)]
        for i in range(tiles):
            for j in range(tiles):
                chosen = zero
                live = zero
                for s in range(slots):
                    match = places[s] == i * tiles + j
                    chosen = jnp.where(match, s, chosen)
                    live = jnp.where(match, 1, live)
                values = tv[q, chosen]
                values = values * jnp.full(values.shape, live, jnp.int32).astype(F32).astype(BF)
                adj[pl.ds(i * tile, tile), pl.ds(k * rows + j * tile, tile)] = values
                adj_t[pl.ds(k * rows + j * tile, tile), pl.ds(i * tile, tile)] = values.T

    nth, row = split(iota((LANES, served), 1), UNIT)
    nth = split(nth, PARTNERS)[1]
    listed = dot(lists, ones_where(nth == iota((LANES, served), 0)))
    for_whom, row = split(iota((blocks, served), 1), PARTNERS * UNIT)
    listed = jnp.where(for_whom == iota((blocks, served), 0), listed, 0.0)
    wanted = jnp.sum(listed, axis=0, keepdims=True)
    wanted = wanted * UNIT + split(iota((1, served), 1), UNIT)[1]
    pick[...] = ones_where(wanted == iota((rows, served), 0))

    bytes_of(2, others(serve_s)).wait_recv()
    away = PARTNERS * rows
    mixed = dot(adj[:, :away], get_rows(serve_r))
    mixed = (mixed + dot(adj[:, away:], regrouped)).astype(BF)
    mixed_r[member] = mixed
    send_members(8, mixed_r.at[member], mixed_r.at[member])
    bytes_of(7, others(w_all)).wait_recv()
    bytes_of(8, others(mixed_r)).wait_recv()

    share = rows // members
    bias_part = jnp.zeros((1, wide), F32)
    for c in range(members):
        part = pl.ds(c * share, share)
        pre = dot(mixed_r[0, part], w_all[0])
        for r in range(1, members):
            pre = pre + dot(mixed_r[r, part], w_all[r])
        pre = pre + bias_ref[...]
        sigma = jax.nn.sigmoid(pre)
        outs[c] = (pre * sigma).astype(BF)
        grad = og_ref[part, :].astype(F32) * sigma * (1.0 + pre * (1.0 - sigma))
        grad = grad.astype(BF)
        pg[part, :] = grad
        bias_part = bias_part + jnp.sum(grad.astype(F32), axis=0, keepdims=True)
        mg[part, :] = dot(grad, w_ref[...], on_lanes).astype(BF)
    out_ref[...] = outs[member]

    put_rows(term_s, dot(adj_t[:away], mg[...]).astype(BF))
    send_all(3, lambda p: term_s.at[:, p], term_r.at[me])
    term_r[me] = term_s[:, me]
    own[...] = dot(adj_t[away:], mg[...])

    weight_part = dot(mixed.T, pg[...])
    groups = wide // LANES
    per_peer = (cols // UNIT) * groups // blocks
    bands = UNIT // groups
    for p in range(blocks):
        for t in range(per_peer):
            band, group = divmod(p * per_peer + t, groups)
            for b in range(bands):
                top = band * UNIT + b * groups
                grad_s[p, t * bands + b] = weight_part[
                    top : top + groups, group * LANES : (group + 1) * LANES
                ]
        for g in range(groups):
            grad_s[p, per_peer * bands, g : g + 1, :] = bias_part[
                :, g * LANES : (g + 1) * LANES
            ]
    send_all(5, lambda p: grad_s.at[p], grad_r.at[me])
    grad_r[me] = grad_s[me]

    bytes_of(3, others(term_r)).wait_recv()
    sums = dot(pick[...], get_rows(term_r))
    put_rows(sum_s, sums.astype(BF))
    send_all(4, lambda p: sum_s.at[p], sum_r.at[me])
    sum_r[me] = sum_s[me]

    bytes_of(5, others(grad_r)).wait_recv()
    total = jnp.sum(grad_r[...], axis=0)
    total_s[...] = total[: per_peer * bands]
    bg_ref[...] = total[per_peer * bands]
    send_all(6, lambda p: total_s, total_r.at[me])
    total_r[me] = total_s[...]

    bytes_of(4, others(sum_r)).wait_recv()
    back = get_rows(sum_r).astype(F32)
    fg_ref[...] = (back + own[...]).astype(BF)

    bytes_of(6, others(total_r)).wait_recv()
    for p in range(blocks):
        for t in range(per_peer):
            band, group = divmod(p * per_peer + t, groups)
            for b in range(bands):
                top = band * UNIT + b * groups
                wg_ref[top : top + groups, group * LANES : (group + 1) * LANES] = total_r[
                    p, t * bands + b
                ]

    bytes_of(0, others(load_s)).wait_send()
    bytes_of(1, others(spread_s)).wait_send()
    bytes_of(2, others(serve_s)).wait_send()
    bytes_of(3, others(term_r)).wait_send()
    bytes_of(4, others(sum_s)).wait_send()
    bytes_of(5, others(grad_s)).wait_send()
    bytes_of(6, others(total_r)).wait_send()
    bytes_of(7, others(w_all)).wait_send()
    bytes_of(8, others(mixed_r)).wait_send()


def per_device(
    features,
    row_target,
    tile_values,
    tile_rows,
    tile_cols,
    tile_counts,
    weight,
    layer_bias,
    out_grad,
):
    blocks = lax.axis_size("blk")
    members = lax.axis_size("rep")
    rows, cols = features.shape
    slots, tile = tile_values.shape[2:4]
    tiles = rows // tile
    bucket = 2 * rows // blocks
    assert rows == blocks * UNIT and cols == LANES and bucket % UNIT == 0
    wide = weight.shape[1]
    groups = wide // LANES
    pieces = (cols // UNIT) * groups // blocks * (UNIT // groups)
    units = bucket // UNIT + 1
    meets = PARTNERS + 1
    slot = lax.broadcasted_iota(jnp.int32, (slots, blocks), 0)
    place = tile_rows[0].T * tiles + tile_cols[0].T
    pos = jnp.where(slot < tile_counts, place, -1)

    vmem = pl.BlockSpec(memory_space=pltpu.VMEM)
    output, weight_grad, bias_grad, feature_grad = pl.pallas_call(
        functools.partial(kernel, blocks, members),
        out_shape=(
            jax.ShapeDtypeStruct((rows // members, wide), BF),
            jax.ShapeDtypeStruct((cols, wide), F32),
            jax.ShapeDtypeStruct((groups, LANES), F32),
            jax.ShapeDtypeStruct((rows, cols), BF),
        ),
        in_specs=[
            vmem,
            vmem,
            pl.BlockSpec(memory_space=pltpu.SMEM),
            pl.BlockSpec(memory_space=pl.ANY),
            vmem,
            vmem,
            vmem,
        ],
        out_specs=(vmem,) * 4,
        scratch_shapes=[
            pltpu.VMEM((blocks, slots, tile, tile), BF),
            pltpu.VMEM((blocks, units, UNIT, LANES), BF),
            pltpu.VMEM((blocks, units, UNIT, LANES), BF),
            pltpu.VMEM((blocks, UNIT, LANES), BF),
            pltpu.VMEM((blocks, UNIT, LANES), BF),
            pltpu.VMEM((PARTNERS * rows, rows), BF),
            pltpu.VMEM((rows, PARTNERS * rows), BF),
            pltpu.VMEM((blocks, PARTNERS, UNIT, LANES), BF),
            pltpu.VMEM((PARTNERS, blocks, UNIT, LANES), BF),
            pltpu.VMEM((rows, meets * rows), BF),
            pltpu.VMEM((meets * rows, rows), BF),
            pltpu.VMEM((members, rows, cols), BF),
            pltpu.VMEM((members, cols, wide), BF),
            pltpu.VMEM((rows, wide), BF),
            pltpu.VMEM((members, rows // members, wide), BF),
            pltpu.VMEM((rows, cols), BF),
            pltpu.VMEM((rows, cols), F32),
            pltpu.VMEM((PARTNERS, blocks, UNIT, LANES), BF),
            pltpu.VMEM((blocks, PARTNERS, UNIT, LANES), BF),
            pltpu.VMEM((blocks, UNIT, LANES), BF),
            pltpu.VMEM((blocks, UNIT, LANES), BF),
            pltpu.VMEM((blocks, pieces + 1, groups, LANES), F32),
            pltpu.VMEM((blocks, pieces + 1, groups, LANES), F32),
            pltpu.VMEM((pieces, groups, LANES), F32),
            pltpu.VMEM((blocks, pieces, groups, LANES), F32),
            pltpu.VMEM((3 * blocks, blocks * units * UNIT), BF),
            pltpu.SemaphoreType.DMA((9,)),
            pltpu.SemaphoreType.DMA((9,)),
            pltpu.SemaphoreType.DMA,
        ],
        compiler_params=pltpu.CompilerParams(
            collective_id=0, has_side_effects=True, vmem_limit_bytes=58 * 2**20
        ),
    )(
        features,
        row_target.reshape(1, rows),
        pos,
        tile_values[0],
        weight,
        layer_bias.reshape(1, wide),
        out_grad,
    )
    return output, weight_grad, bias_grad.reshape(wide), feature_grad


def solution(mesh):
    in_specs = (
        P("blk", "rep"),
        P("blk"),
        P("blk", None, None, None, None),
        P("blk", None, None),
        P("blk", None, None),
        P("blk", None),
        P("rep", None),
        P(),
        P("blk", None),
    )
    out_specs = (P(("blk", "rep"), None), P("rep", None), P(), P("blk", "rep"))
    return jax.shard_map(
        per_device, mesh=mesh, in_specs=in_specs, out_specs=out_specs, check_vma=False
    )
```

```python
import functools
import math

import jax
import jax.numpy as jnp
from jax import lax
from jax.experimental import pallas as pl
from jax.experimental.pallas import tpu as pltpu
from jax.sharding import PartitionSpec as P

PARTNERS = 6
BF = jnp.bfloat16
F32 = jnp.float32
MESH = pl.DeviceIdType.MESH
LANES = 128
UNIT = 8
LINE = 8
PIECE = 16
KINDS = 4


def dot(a, b, dims=((1,), (0,))):
    return lax.dot_general(a, b, (dims, ((), ())), preferred_element_type=F32)


def iota(shape, dim):
    return lax.broadcasted_iota(jnp.int32, shape, dim).astype(F32)


def split(x, by):
    whole = jnp.floor((x + 0.5) * (1.0 / by))
    return whole, x - whole * by


def as_rows(ref):
    return ref.reshape(math.prod(ref.shape[:-1]), ref.shape[-1])


def get_rows(ref):
    return as_rows(ref)[...]


def put_rows(ref, value):
    as_rows(ref)[...] = value


def step_to(kind, across):
    return (0, 1, -1, 2 - 4 * (across % 2))[kind]


def ones_where(condition):
    return jnp.where(condition, 1.0, 0.0).astype(BF)


def kernel(
    blocks,
    members,
    feat,
    target_ref,
    pos,
    tile_hbm,
    w_ref,
    bias_ref,
    og_ref,
    out_ref,
    wg_ref,
    bg_ref,
    fg_ref,
    tv,
    load_s,
    load_r,
    spread_s,
    spread_r,
    pick_t,
    pick,
    serve_s,
    serve_r,
    adj,
    adj_t,
    mixed_r,
    w_all,
    pg,
    outs,
    mg,
    own,
    term_s,
    term_r,
    sum_s,
    sum_r,
    grad_s,
    grad_r,
    total_s,
    total_r,
    find,
    offset,
    bias_s,
    send_sem,
    recv_sem,
    tile_sem,
):
    me = lax.axis_index("blk")
    member = lax.axis_index("rep")
    rows, cols = feat.shape
    slots, tile = tv.shape[1:3]
    tiles = rows // tile
    bucket = 2 * rows // blocks
    wide = w_ref.shape[1]
    unit_rows = bucket + UNIT
    loaded = blocks * unit_rows
    lines = blocks // LINE
    across = lax.div(me, LINE)
    along = lax.rem(me, LINE)
    half = LINE // 2
    my_class = across * half + lax.rem(along, half)
    near = lines * KINDS
    served = near * PARTNERS * PIECE
    held = blocks * PIECE
    meets = PARTNERS + 1

    load_tiles = pltpu.make_async_copy(tile_hbm, tv, tile_sem)
    load_tiles.start()
    barrier = pltpu.get_barrier_semaphore()

    def greet(d, _):
        pl.semaphore_signal(
            barrier, inc=1, device_id=(lax.rem(me + d, blocks), member), device_id_type=MESH
        )
        return 0

    lax.fori_loop(1, blocks, greet, 0)
    for d in range(1, members):
        pl.semaphore_signal(
            barrier, inc=1, device_id=(me, lax.rem(member + d, members)), device_id_type=MESH
        )

    def send_all(phase, source, dest):
        def one(d, _):
            peer = lax.rem(me + d, blocks)
            pltpu.make_async_remote_copy(
                src_ref=source(peer),
                dst_ref=dest,
                send_sem=send_sem.at[phase],
                recv_sem=recv_sem.at[phase],
                device_id=(peer, member),
                device_id_type=MESH,
            ).start()
            return 0

        lax.fori_loop(1, blocks, one, 0)

    def whom(index):
        turn, kind = split(index, KINDS)
        to = turn + across.astype(F32)
        to = jnp.where(to >= lines, to - lines, to)
        far = 2.0 - 4.0 * split(to, 2)[1]
        step = jnp.where(kind == 1, 1.0, jnp.where(kind == 2, -1.0, far))
        at = jnp.where(kind == 0, 0.0, step) + along.astype(F32)
        at = jnp.where(at < 0, at + LINE, at)
        at = jnp.where(at >= LINE, at - LINE, at)
        return to * LINE + at

    def send_near(phase, make):
        for kind in range(KINDS):

            def one(turn, _, kind=kind):
                peer, source, dest = make(turn, kind)
                pltpu.make_async_remote_copy(
                    src_ref=source,
                    dst_ref=dest,
                    send_sem=send_sem.at[phase],
                    recv_sem=recv_sem.at[phase],
                    device_id=(peer, member),
                    device_id_type=MESH,
                ).start()
                return 0

            lax.fori_loop(1 if kind == 0 else 0, lines, one, 0)

    def serve(turn, kind):
        to = lax.rem(across + turn, lines)
        at = lax.rem(along + step_to(kind, to) + LINE, LINE)
        return to * LINE + at, serve_s.at[turn * KINDS + kind], serve_r.at[:, my_class]

    def give_back(turn, kind):
        to = lax.rem(across + turn, lines)
        at = lax.rem(along - step_to(kind, across) + LINE, LINE)
        place = lax.rem(lines - turn, lines) * KINDS + kind
        held_class = to * half + lax.rem(at, half)
        return to * LINE + at, term_s.at[:, held_class], term_r.at[place]

    def send_members(phase, source, dest):
        for d in range(1, members):
            pltpu.make_async_remote_copy(
                src_ref=source,
                dst_ref=dest,
                send_sem=send_sem.at[phase],
                recv_sem=recv_sem.at[phase],
                device_id=(me, lax.rem(member + d, members)),
                device_id_type=MESH,
            ).start()

    def bytes_of(phase, ref):
        return pltpu.make_async_remote_copy(
            src_ref=ref,
            dst_ref=ref,
            send_sem=send_sem.at[phase],
            recv_sem=recv_sem.at[phase],
            device_id=(me, member),
            device_id_type=MESH,
        )

    def others(ref):
        return ref.at[pl.ds(0, ref.shape[0] - 1)]

    def scan(q, state):
        count, found = state
        live = (pos[0, q] >= 0) & (q != me)
        found = tuple(
            jnp.where(live & (count == k), q, f) for k, f in enumerate(found)
        )
        return count + jnp.where(live, 1, 0), found

    zero = jnp.int32(0)
    _, partners = lax.fori_loop(0, blocks, scan, (zero, (zero,) * PARTNERS))

    target = target_ref[...]
    goal, landing = split(target.astype(F32), rows)
    hits = ones_where(goal == iota((blocks, rows), 0))
    before = ones_where(iota((rows, rows), 0) < iota((rows, rows), 1))
    earlier = dot(hits, before)
    rank = jnp.sum(hits.astype(F32) * earlier, axis=0, keepdims=True)
    high, low = split(landing + 1.0, 16)
    of_rank = ones_where(rank == iota((LANES, rows), 0))
    on_lanes = ((1,), (1,))
    land_high = dot(hits * high.astype(BF), of_rank, on_lanes)
    land_low = dot(hits * low.astype(BF), of_rank, on_lanes)
    lane = lax.broadcasted_iota(jnp.int32, (blocks, LANES), 1)
    listed = jnp.zeros((blocks, LANES), jnp.int32)
    for k in range(PARTNERS):
        listed = jnp.where(lane == k, partners[k], listed)
    notes = jnp.concatenate([land_high, land_low, listed.astype(F32)], axis=0).astype(BF)
    to_unit = ones_where(goal * unit_rows + rank == iota((loaded, rows), 0))
    n_notes = 3 * blocks
    unit, inside = split(iota((loaded, n_notes), 0), unit_rows)
    kind, whose = split(iota((loaded, n_notes), 1), blocks)
    to_note = ones_where((unit == whose) & (inside == kind + bucket))
    filled = dot(to_unit, feat[...]) + dot(to_note, notes)
    put_rows(load_s, filled.astype(BF))

    pl.semaphore_wait(barrier, blocks + members - 2)
    send_all(0, lambda p: load_s.at[p], load_r.at[me])
    send_members(7, w_ref, w_all.at[member])
    load_r[me] = load_s[me]
    w_all[member] = w_ref[...]
    unit, inside = split(iota((n_notes, loaded), 1), unit_rows)
    kind, whose = split(iota((n_notes, loaded), 0), blocks)
    find[...] = ones_where((unit == whose) & (inside == kind + bucket))
    shift = split(iota(offset.shape, 0), PIECE)[1]
    offset[...] = iota(offset.shape, 1) - shift
    bytes_of(0, others(load_r)).wait_recv()

    got = get_rows(load_r)
    notes = dot(find[...], got)
    unit, inside = split(iota((blocks, loaded), 1), unit_rows)
    fold = ones_where(iota((LANES, loaded), 0) == split(iota((LANES, loaded), 1), unit_rows)[1])
    lands = 16.0 * dot(notes[:blocks].astype(BF), fold) + dot(
        notes[blocks : 2 * blocks].astype(BF), fold
    )
    lands = jnp.where(unit == iota((blocks, loaded), 0), lands, 0.0)
    lands = jnp.sum(lands, axis=0, keepdims=True) - 1.0
    regroup = ones_where(lands == iota((rows, loaded), 0))
    regrouped = dot(regroup, got).astype(BF)
    put_rows(spread_s, regrouped)

    def class_of(peer):
        return lax.div(peer, LINE) * half + lax.rem(lax.rem(peer, LINE), half)

    send_all(1, lambda p: spread_s.at[class_of(p)], spread_r.at[me])
    spread_r[me] = spread_s[my_class]

    lists = notes[2 * blocks :].astype(BF)
    chunk = rows

    def fill_pick_t(i, _):
        first = (i * chunk).astype(F32)
        place = split(iota((chunk, blocks), 0) + first, PARTNERS * PIECE)[0]
        for_whom = ones_where(whom(place) == iota((chunk, blocks), 1))
        nth = split(iota((chunk, LANES), 0) + first, PIECE)[0]
        nth = split(nth, PARTNERS)[1]
        listed = jnp.where(nth == iota((chunk, LANES), 1), dot(for_whom, lists), 0.0)
        wanted = dot(listed.astype(BF), jnp.full((LANES, held), PIECE, BF))
        match = ones_where(wanted == offset[...])
        pick_t[pl.ds(pl.multiple_of(i * chunk, chunk), chunk), :] = match
        return 0

    lax.fori_loop(0, served // chunk, fill_pick_t, 0)
    bytes_of(1, others(spread_r)).wait_recv()
    put_rows(serve_s, dot(pick_t[...], get_rows(spread_r)).astype(BF))
    send_near(2, serve)
    serve_r[:, my_class] = serve_s[0]

    load_tiles.wait()
    for k in range(meets):
        q = me if k == PARTNERS else partners[k]
        places = [pos[s, q] for s in range(slots)]
        for i in range(tiles):
            for j in range(tiles):
                chosen = zero
                live = zero
                for s in range(slots):
                    match = places[s] == i * tiles + j
                    chosen = jnp.where(match, s, chosen)
                    live = jnp.where(match, 1, live)
                values = tv[q, chosen]
                values = values * jnp.full(values.shape, live, jnp.int32).astype(F32).astype(BF)
                adj[pl.ds(i * tile, tile), pl.ds(k * rows + j * tile, tile)] = values
                adj_t[pl.ds(k * rows + j * tile, tile), pl.ds(i * tile, tile)] = values.T

    nth = split(iota((LANES, served), 1), PIECE)[0]
    nth = split(nth, PARTNERS)[1]
    listed = dot(lists, ones_where(nth == iota((LANES, served), 0)))
    place = split(iota((1, served), 1), PARTNERS * PIECE)[0]
    listed = jnp.where(whom(place) == iota((blocks, served), 0), listed, 0.0)
    wanted = jnp.sum(listed, axis=0, keepdims=True)
    wanted = wanted * PIECE + split(iota((1, served), 1), PIECE)[1]
    part_rows = held // KINDS
    for c in range(KINDS):
        at = iota((part_rows, served), 0) + float(c * part_rows)
        pick[pl.ds(c * part_rows, part_rows), :] = ones_where(wanted == at)

    bytes_of(2, others(serve_s)).wait_recv()
    away = PARTNERS * rows
    mixed = dot(adj[:, :away], get_rows(serve_r))
    mixed = (mixed + dot(adj[:, away:], regrouped)).astype(BF)
    mixed_r[member] = mixed
    send_members(8, mixed_r.at[member], mixed_r.at[member])
    bytes_of(7, others(w_all)).wait_recv()
    bytes_of(8, others(mixed_r)).wait_recv()

    share = rows // members
    bias_part = jnp.zeros((1, wide), F32)
    for c in range(members):
        part = pl.ds(c * share, share)
        pre = dot(mixed_r[0, part], w_all[0])
        for r in range(1, members):
            pre = pre + dot(mixed_r[r, part], w_all[r])
        pre = pre + bias_ref[...]
        sigma = jax.nn.sigmoid(pre)
        outs[c] = (pre * sigma).astype(BF)
        grad = og_ref[part, :].astype(F32) * sigma * (1.0 + pre * (1.0 - sigma))
        grad = grad.astype(BF)
        pg[part, :] = grad
        bias_part = bias_part + jnp.sum(grad.astype(F32), axis=0, keepdims=True)
        mg[part, :] = dot(grad, w_ref[...], on_lanes).astype(BF)
    out_ref[...] = outs[member]

    put_rows(term_s, dot(adj_t[:away], mg[...]).astype(BF))
    send_near(3, give_back)
    term_r[0] = term_s[:, my_class]
    own[...] = dot(adj_t[away:], mg[...])

    weight_part = dot(mixed.T, pg[...])
    groups = wide // LANES
    per_peer = (cols // UNIT) * groups // blocks
    bias_s[...] = jnp.zeros(bias_s.shape, F32)
    for g in range(groups):
        exact = bias_part[:, g * LANES : (g + 1) * LANES]
        rounded = exact.astype(BF).astype(F32)
        bias_s[g : g + 1, :] = rounded
        bias_s[groups + g : groups + g + 1, :] = exact - rounded
    bias_rows = bias_s[...].astype(BF)
    for p in range(blocks):
        for t in range(per_peer):
            band, group = divmod(p * per_peer + t, groups)
            grad_s[p, t] = weight_part[
                band * UNIT : (band + 1) * UNIT, group * LANES : (group + 1) * LANES
            ].astype(BF)
        grad_s[p, per_peer] = bias_rows
    send_all(5, lambda p: grad_s.at[p], grad_r.at[me])
    grad_r[me] = grad_s[me]

    bytes_of(3, others(term_r)).wait_recv()
    sums = dot(pick[...], get_rows(term_r))
    put_rows(sum_s, sums.astype(BF))
    send_all(4, lambda p: sum_s.at[p], sum_r.at[me])
    sum_r[me] = sum_s[me]

    bytes_of(5, others(grad_r)).wait_recv()
    total = grad_r[0].astype(F32)
    for p in range(1, blocks):
        total = total + grad_r[p].astype(F32)
    total_s[...] = total[:per_peer].astype(BF)
    bg_ref[...] = total[per_peer, :groups] + total[per_peer, groups : 2 * groups]
    send_all(6, lambda p: total_s, total_r.at[me])
    total_r[me] = total_s[...]

    bytes_of(4, others(sum_r)).wait_recv()
    stretch = half * PIECE
    for a in range(lines):
        for side in range(2):
            for c in range(half):
                where = pl.ds(a * stretch + c * PIECE, PIECE)
                own[where, :] += sum_r[a * LINE + side * half + c].astype(F32)
    fg_ref[...] = own[...].astype(BF)

    bytes_of(6, others(total_r)).wait_recv()
    for p in range(blocks):
        for t in range(per_peer):
            band, group = divmod(p * per_peer + t, groups)
            wg_ref[
                band * UNIT : (band + 1) * UNIT, group * LANES : (group + 1) * LANES
            ] = total_r[p, t].astype(F32)

    bytes_of(0, others(load_s)).wait_send()
    bytes_of(1, others(spread_r)).wait_send()
    bytes_of(2, others(serve_s)).wait_send()
    bytes_of(3, others(term_r)).wait_send()
    bytes_of(4, others(sum_s)).wait_send()
    bytes_of(5, others(grad_s)).wait_send()
    bytes_of(6, others(total_r)).wait_send()
    bytes_of(7, others(w_all)).wait_send()
    bytes_of(8, others(mixed_r)).wait_send()


def hand_over(*refs):
    for source, dest in zip(refs[: len(refs) // 2], refs[len(refs) // 2 :]):
        dest[...] = source[...]


def per_device(
    features,
    row_target,
    tile_values,
    tile_rows,
    tile_cols,
    tile_counts,
    weight,
    layer_bias,
    out_grad,
):
    blocks = lax.axis_size("blk")
    members = lax.axis_size("rep")
    rows, cols = features.shape
    slots, tile = tile_values.shape[2:4]
    tiles = rows // tile
    bucket = 2 * rows // blocks
    assert rows == blocks * UNIT and cols == LANES and bucket % UNIT == 0
    wide = weight.shape[1]
    groups = wide // LANES
    pieces = (cols // UNIT) * groups // blocks
    half = blocks // 2
    held = blocks * PIECE
    away = PARTNERS * rows
    units = bucket // UNIT + 1
    meets = PARTNERS + 1
    slot = lax.broadcasted_iota(jnp.int32, (slots, blocks), 0)
    place = tile_rows[0].T * tiles + tile_cols[0].T
    pos = jnp.where(slot < tile_counts, place, -1)

    vmem = pl.BlockSpec(memory_space=pltpu.VMEM)
    results = pl.pallas_call(
        functools.partial(kernel, blocks, members),
        out_shape=(
            jax.ShapeDtypeStruct((rows // members, wide), BF),
            jax.ShapeDtypeStruct((cols, wide), F32),
            jax.ShapeDtypeStruct((groups, LANES), F32),
            jax.ShapeDtypeStruct((rows, cols), BF),
        ),
        in_specs=[
            vmem,
            vmem,
            pl.BlockSpec(memory_space=pltpu.SMEM),
            pl.BlockSpec(memory_space=pl.ANY),
            vmem,
            vmem,
            vmem,
        ],
        out_specs=(vmem,) * 4,
        scratch_shapes=[
            pltpu.VMEM((blocks, slots, tile, tile), BF),
            pltpu.VMEM((blocks, units, UNIT, LANES), BF),
            pltpu.VMEM((blocks, units, UNIT, LANES), BF),
            pltpu.VMEM((half, PIECE, LANES), BF),
            pltpu.VMEM((blocks, PIECE, LANES), BF),
            pltpu.VMEM((away, held), BF),
            pltpu.VMEM((held, away), BF),
            pltpu.VMEM((half, PARTNERS, PIECE, LANES), BF),
            pltpu.VMEM((PARTNERS, half, PIECE, LANES), BF),
            pltpu.VMEM((rows, meets * rows), BF),
            pltpu.VMEM((meets * rows, rows), BF),
            pltpu.VMEM((members, rows, cols), BF),
            pltpu.VMEM((members, cols, wide), BF),
            pltpu.VMEM((rows, wide), BF),
            pltpu.VMEM((members, rows // members, wide), BF),
            pltpu.VMEM((rows, cols), BF),
            pltpu.VMEM((rows, cols), F32),
            pltpu.VMEM((PARTNERS, half, PIECE, LANES), BF),
            pltpu.VMEM((half, PARTNERS, PIECE, LANES), BF),
            pltpu.VMEM((blocks, PIECE, LANES), BF),
            pltpu.VMEM((blocks, PIECE, LANES), BF),
            pltpu.VMEM((blocks, pieces + 1, UNIT, LANES), BF),
            pltpu.VMEM((blocks, pieces + 1, UNIT, LANES), BF),
            pltpu.VMEM((pieces, UNIT, LANES), BF),
            pltpu.VMEM((blocks, pieces, UNIT, LANES), BF),
            pltpu.VMEM((3 * blocks, blocks * units * UNIT), BF),
            pltpu.VMEM((rows, held), F32),
            pltpu.VMEM((UNIT, LANES), F32),
            pltpu.SemaphoreType.DMA((9,)),
            pltpu.SemaphoreType.DMA((9,)),
            pltpu.SemaphoreType.DMA,
        ],
        compiler_params=pltpu.CompilerParams(
            collective_id=0, has_side_effects=True, vmem_limit_bytes=58 * 2**20
        ),
    )(
        features,
        row_target.reshape(1, rows),
        pos,
        tile_values[0],
        weight,
        layer_bias.reshape(1, wide),
        out_grad,
    )
    output, weight_grad, bias_grad, feature_grad = pl.pallas_call(
        hand_over,
        out_shape=tuple(jax.ShapeDtypeStruct(r.shape, r.dtype) for r in results),
        in_specs=[vmem] * len(results),
        out_specs=(vmem,) * len(results),
    )(*results)
    return output, weight_grad, bias_grad.reshape(wide), feature_grad


def solution(mesh):
    in_specs = (
        P("blk", "rep"),
        P("blk"),
        P("blk", None, None, None, None),
        P("blk", None, None),
        P("blk", None, None),
        P("blk", None),
        P("rep", None),
        P(),
        P("blk", None),
    )
    out_specs = (P(("blk", "rep"), None), P("rep", None), P(), P("blk", "rep"))
    return jax.shard_map(
        per_device, mesh=mesh, in_specs=in_specs, out_specs=out_specs, check_vma=False
    )
```

```python
import functools
import math

import jax
import jax.numpy as jnp
from jax import lax
from jax.experimental import pallas as pl
from jax.experimental.pallas import tpu as pltpu
from jax.sharding import PartitionSpec as P

PARTNERS = 6
BF = jnp.bfloat16
F32 = jnp.float32
MESH = pl.DeviceIdType.MESH
LANES = 128
UNIT = 8
LINE = 8
PIECE = 16
KINDS = 4


def dot(a, b, dims=((1,), (0,))):
    return lax.dot_general(a, b, (dims, ((), ())), preferred_element_type=F32)


def iota(shape, dim):
    return lax.broadcasted_iota(jnp.int32, shape, dim).astype(F32)


def split(x, by):
    whole = jnp.floor((x + 0.5) * (1.0 / by))
    return whole, x - whole * by


def as_rows(ref):
    return ref.reshape(math.prod(ref.shape[:-1]), ref.shape[-1])


def get_rows(ref):
    return as_rows(ref)[...]


def put_rows(ref, value):
    as_rows(ref)[...] = value


def put_part(ref, first, count, value):
    size = math.prod(ref.shape[1:-1])
    start = pl.multiple_of(first * size, count * size)
    as_rows(ref)[pl.ds(start, count * size), :] = value


def step_to(kind, across):
    return (0, 1, -1, 2 - 4 * (across % 2))[kind]


def ones_where(condition):
    return jnp.where(condition, 1.0, 0.0).astype(BF)


def kernel(
    blocks,
    members,
    feat,
    target_ref,
    pos,
    tile_hbm,
    w_ref,
    bias_ref,
    og_ref,
    out_ref,
    wg_ref,
    bg_ref,
    fg_ref,
    tv,
    load_s,
    load_r,
    spread_s,
    spread_r,
    pick_t,
    pick,
    serve_s,
    serve_r,
    adj,
    adj_t,
    mixed_r,
    w_all,
    pg,
    outs,
    mg,
    own,
    term_s,
    term_r,
    sum_s,
    sum_r,
    grad_s,
    grad_r,
    total_s,
    total_r,
    find,
    offset,
    bias_s,
    send_sem,
    recv_sem,
    tile_sem,
):
    me = lax.axis_index("blk")
    member = lax.axis_index("rep")
    rows, cols = feat.shape
    slots, tile = tv.shape[1:3]
    tiles = rows // tile
    bucket = 2 * rows // blocks
    wide = w_ref.shape[1]
    unit_rows = bucket + UNIT
    loaded = blocks * unit_rows
    lines = blocks // LINE
    across = lax.div(me, LINE)
    along = lax.rem(me, LINE)
    half = LINE // 2
    my_class = across * half + lax.rem(along, half)
    near = lines * KINDS
    served = near * PARTNERS * PIECE
    held = blocks * PIECE
    meets = PARTNERS + 1

    load_tiles = pltpu.make_async_copy(tile_hbm, tv, tile_sem)
    load_tiles.start()
    barrier = pltpu.get_barrier_semaphore()

    def greet(d, _):
        pl.semaphore_signal(
            barrier, inc=1, device_id=(lax.rem(me + d, blocks), member), device_id_type=MESH
        )
        return 0

    lax.fori_loop(1, blocks, greet, 0)
    for d in range(1, members):
        pl.semaphore_signal(
            barrier, inc=1, device_id=(me, lax.rem(member + d, members)), device_id_type=MESH
        )

    def send_all(phase, source, dest):
        def one(d, _):
            peer = lax.rem(me + d, blocks)
            pltpu.make_async_remote_copy(
                src_ref=source(peer),
                dst_ref=dest,
                send_sem=send_sem.at[phase],
                recv_sem=recv_sem.at[phase],
                device_id=(peer, member),
                device_id_type=MESH,
            ).start()
            return 0

        lax.fori_loop(1, blocks, one, 0)

    def whom(index):
        turn, kind = split(index, KINDS)
        to = turn + across.astype(F32)
        to = jnp.where(to >= lines, to - lines, to)
        far = 2.0 - 4.0 * split(to, 2)[1]
        step = jnp.where(kind == 1, 1.0, jnp.where(kind == 2, -1.0, far))
        at = jnp.where(kind == 0, 0.0, step) + along.astype(F32)
        at = jnp.where(at < 0, at + LINE, at)
        at = jnp.where(at >= LINE, at - LINE, at)
        return to * LINE + at

    def start(phase, peer, source, dest):
        pltpu.make_async_remote_copy(
            src_ref=source,
            dst_ref=dest,
            send_sem=send_sem.at[phase],
            recv_sem=recv_sem.at[phase],
            device_id=(peer, member),
            device_id_type=MESH,
        ).start()

    def serve(turn, kind):
        to = lax.rem(across + turn, lines)
        at = lax.rem(along + step_to(kind, to) + LINE, LINE)
        return to * LINE + at, serve_s.at[turn * KINDS + kind], serve_r.at[:, my_class]

    def give_back(turn, kind):
        to = lax.rem(across + turn, lines)
        at = lax.rem(along - step_to(kind, across) + LINE, LINE)
        place = lax.rem(lines - turn, lines) * KINDS + kind
        held_class = to * half + lax.rem(at, half)
        return to * LINE + at, term_s.at[:, held_class], term_r.at[place]

    def send_members(phase, source, dest):
        for d in range(1, members):
            pltpu.make_async_remote_copy(
                src_ref=source,
                dst_ref=dest,
                send_sem=send_sem.at[phase],
                recv_sem=recv_sem.at[phase],
                device_id=(me, lax.rem(member + d, members)),
                device_id_type=MESH,
            ).start()

    def bytes_of(phase, ref):
        return pltpu.make_async_remote_copy(
            src_ref=ref,
            dst_ref=ref,
            send_sem=send_sem.at[phase],
            recv_sem=recv_sem.at[phase],
            device_id=(me, member),
            device_id_type=MESH,
        )

    def others(ref):
        return ref.at[pl.ds(0, ref.shape[0] - 1)]

    def scan(q, state):
        count, found = state
        live = (pos[0, q] >= 0) & (q != me)
        found = tuple(
            jnp.where(live & (count == k), q, f) for k, f in enumerate(found)
        )
        return count + jnp.where(live, 1, 0), found

    zero = jnp.int32(0)
    _, partners = lax.fori_loop(0, blocks, scan, (zero, (zero,) * PARTNERS))

    target = target_ref[...]
    goal, landing = split(target.astype(F32), rows)
    hits = ones_where(goal == iota((blocks, rows), 0))
    before = ones_where(iota((rows, rows), 0) < iota((rows, rows), 1))
    earlier = dot(hits, before)
    rank = jnp.sum(hits.astype(F32) * earlier, axis=0, keepdims=True)
    high, low = split(landing + 1.0, 16)
    of_rank = ones_where(rank == iota((LANES, rows), 0))
    on_lanes = ((1,), (1,))
    land_high = dot(hits * high.astype(BF), of_rank, on_lanes)
    land_low = dot(hits * low.astype(BF), of_rank, on_lanes)
    lane = lax.broadcasted_iota(jnp.int32, (blocks, LANES), 1)
    listed = jnp.zeros((blocks, LANES), jnp.int32)
    for k in range(PARTNERS):
        listed = jnp.where(lane == k, partners[k], listed)
    notes = jnp.concatenate([land_high, land_low, listed.astype(F32)], axis=0).astype(BF)
    to_unit = ones_where(goal * unit_rows + rank == iota((loaded, rows), 0))
    n_notes = 3 * blocks
    unit, inside = split(iota((loaded, n_notes), 0), unit_rows)
    kind, whose = split(iota((loaded, n_notes), 1), blocks)
    to_note = ones_where((unit == whose) & (inside == kind + bucket))
    filled = dot(to_unit, feat[...]) + dot(to_note, notes)
    put_rows(load_s, filled.astype(BF))

    pl.semaphore_wait(barrier, blocks + members - 2)
    send_all(0, lambda p: load_s.at[p], load_r.at[me])
    send_members(7, w_ref, w_all.at[member])
    load_r[me] = load_s[me]
    w_all[member] = w_ref[...]
    unit, inside = split(iota((n_notes, loaded), 1), unit_rows)
    kind, whose = split(iota((n_notes, loaded), 0), blocks)
    find[...] = ones_where((unit == whose) & (inside == kind + bucket))
    shift = split(iota(offset.shape, 0), PIECE)[1]
    offset[...] = iota(offset.shape, 1) - shift
    bytes_of(0, others(load_r)).wait_recv()

    got = get_rows(load_r)
    notes = dot(find[...], got)
    unit, inside = split(iota((blocks, loaded), 1), unit_rows)
    fold = ones_where(iota((LANES, loaded), 0) == split(iota((LANES, loaded), 1), unit_rows)[1])
    lands = 16.0 * dot(notes[:blocks].astype(BF), fold) + dot(
        notes[blocks : 2 * blocks].astype(BF), fold
    )
    lands = jnp.where(unit == iota((blocks, loaded), 0), lands, 0.0)
    lands = jnp.sum(lands, axis=0, keepdims=True) - 1.0
    regroup = ones_where(lands == iota((rows, loaded), 0))
    regrouped = dot(regroup, got).astype(BF)
    put_rows(spread_s, regrouped)

    def class_of(peer):
        return lax.div(peer, LINE) * half + lax.rem(lax.rem(peer, LINE), half)

    send_all(1, lambda p: spread_s.at[class_of(p)], spread_r.at[me])
    spread_r[me] = spread_s[my_class]

    lists = notes[2 * blocks :].astype(BF)
    chunk = rows

    def fill_pick_t(i, _):
        first = (i * chunk).astype(F32)
        place = split(iota((chunk, blocks), 0) + first, PARTNERS * PIECE)[0]
        for_whom = ones_where(whom(place) == iota((chunk, blocks), 1))
        nth = split(iota((chunk, LANES), 0) + first, PIECE)[0]
        nth = split(nth, PARTNERS)[1]
        listed = jnp.where(nth == iota((chunk, LANES), 1), dot(for_whom, lists), 0.0)
        wanted = dot(listed.astype(BF), jnp.full((LANES, held), PIECE, BF))
        match = ones_where(wanted == offset[...])
        pick_t[pl.ds(pl.multiple_of(i * chunk, chunk), chunk), :] = match
        return 0

    lax.fori_loop(0, served // chunk, fill_pick_t, 0)
    bytes_of(1, others(spread_r)).wait_recv()
    turn_rows = KINDS * PARTNERS * PIECE

    def serve_turn(turn, _):
        part = pl.ds(pl.multiple_of(turn * turn_rows, turn_rows), turn_rows)
        pieces = dot(pick_t[part, :], get_rows(spread_r)).astype(BF)
        put_part(serve_s, turn * KINDS, KINDS, pieces)
        for kind in range(KINDS):
            start(2, *serve(turn, kind))
        return 0

    pieces = dot(pick_t[:turn_rows, :], get_rows(spread_r)).astype(BF)
    put_part(serve_s, 0, KINDS, pieces)
    for kind in range(1, KINDS):
        start(2, *serve(0, kind))
    lax.fori_loop(1, lines, serve_turn, 0)
    serve_r[:, my_class] = serve_s[0]

    load_tiles.wait()
    for k in range(meets):
        q = me if k == PARTNERS else partners[k]
        places = [pos[s, q] for s in range(slots)]
        for i in range(tiles):
            for j in range(tiles):
                chosen = zero
                live = zero
                for s in range(slots):
                    match = places[s] == i * tiles + j
                    chosen = jnp.where(match, s, chosen)
                    live = jnp.where(match, 1, live)
                values = tv[q, chosen]
                values = values * jnp.full(values.shape, live, jnp.int32).astype(F32).astype(BF)
                adj[pl.ds(i * tile, tile), pl.ds(k * rows + j * tile, tile)] = values
                adj_t[pl.ds(k * rows + j * tile, tile), pl.ds(i * tile, tile)] = values.T

    nth = split(iota((LANES, served), 1), PIECE)[0]
    nth = split(nth, PARTNERS)[1]
    listed = dot(lists, ones_where(nth == iota((LANES, served), 0)))
    place = split(iota((1, served), 1), PARTNERS * PIECE)[0]
    listed = jnp.where(whom(place) == iota((blocks, served), 0), listed, 0.0)
    wanted = jnp.sum(listed, axis=0, keepdims=True)
    wanted = wanted * PIECE + split(iota((1, served), 1), PIECE)[1]
    part_rows = held // KINDS
    for c in range(KINDS):
        at = iota((part_rows, served), 0) + float(c * part_rows)
        pick[pl.ds(c * part_rows, part_rows), :] = ones_where(wanted == at)

    bytes_of(2, others(serve_s)).wait_recv()
    away = PARTNERS * rows
    share = rows // members
    for c in range(members):
        part = pl.ds(c * share, share)
        mixed = dot(adj[part, :away], get_rows(serve_r)) + dot(adj[part, away:], regrouped)
        mixed_r[member, part] = mixed.astype(BF)
        send_members(8 + c, mixed_r.at[member, part], mixed_r.at[member, part])
    bytes_of(7, others(w_all)).wait_recv()
    some = mixed_r.at[pl.ds(0, members - 1), pl.ds(0, share)]

    bias_part = jnp.zeros((1, wide), F32)
    for c in range(members):
        part = pl.ds(c * share, share)
        bytes_of(8 + c, some).wait_recv()
        pre = dot(mixed_r[0, part], w_all[0])
        for r in range(1, members):
            pre = pre + dot(mixed_r[r, part], w_all[r])
        pre = pre + bias_ref[...]
        sigma = jax.nn.sigmoid(pre)
        outs[c] = (pre * sigma).astype(BF)
        grad = og_ref[part, :].astype(F32) * sigma * (1.0 + pre * (1.0 - sigma))
        grad = grad.astype(BF)
        pg[part, :] = grad
        bias_part = bias_part + jnp.sum(grad.astype(F32), axis=0, keepdims=True)
        mg[part, :] = dot(grad, w_ref[...], on_lanes).astype(BF)
    out_ref[...] = outs[member]

    put_rows(term_s, dot(adj_t[:away], mg[...]).astype(BF))
    for kind in range(1, KINDS):
        start(3, *give_back(0, kind))

    def give_turn(turn, _):
        for kind in range(KINDS):
            start(3, *give_back(turn, kind))
        return 0

    lax.fori_loop(1, lines, give_turn, 0)
    term_r[0] = term_s[:, my_class]
    own[...] = dot(adj_t[away:], mg[...])

    weight_part = dot(mixed_r[member].T, pg[...])
    groups = wide // LANES
    per_peer = (cols // UNIT) * groups // blocks
    bias_s[...] = jnp.zeros(bias_s.shape, F32)
    for g in range(groups):
        exact = bias_part[:, g * LANES : (g + 1) * LANES]
        rounded = exact.astype(BF).astype(F32)
        bias_s[g : g + 1, :] = rounded
        bias_s[groups + g : groups + g + 1, :] = exact - rounded
    bias_rows = bias_s[...].astype(BF)
    for p in range(blocks):
        for t in range(per_peer):
            band, group = divmod(p * per_peer + t, groups)
            grad_s[p, t] = weight_part[
                band * UNIT : (band + 1) * UNIT, group * LANES : (group + 1) * LANES
            ].astype(BF)
        grad_s[p, per_peer] = bias_rows
    send_all(5, lambda p: grad_s.at[p], grad_r.at[me])
    grad_r[me] = grad_s[me]

    bytes_of(3, others(term_r)).wait_recv()
    some_lines = max(1, lines // 4)
    together = some_lines * LINE
    for turn in range(lines // some_lines):
        line = lax.rem(lax.div(across, some_lines) * some_lines + turn * some_lines, lines)
        part = pl.ds(pl.multiple_of(line * LINE * PIECE, together * PIECE), together * PIECE)
        sums = dot(pick[part, :], get_rows(term_r)).astype(BF)
        put_part(sum_s, line * LINE, together, sums)

        def hand_back(d, _, line=line):
            peer = line * LINE + lax.rem(me + d, together)
            start(4, peer, sum_s.at[peer], sum_r.at[me])
            return 0

        lax.fori_loop(1 if turn == 0 else 0, together, hand_back, 0)
    sum_r[me] = sum_s[me]

    bytes_of(5, others(grad_r)).wait_recv()
    total = grad_r[0].astype(F32)
    for p in range(1, blocks):
        total = total + grad_r[p].astype(F32)
    total_s[...] = total[:per_peer].astype(BF)
    bg_ref[...] = total[per_peer, :groups] + total[per_peer, groups : 2 * groups]
    send_all(6, lambda p: total_s, total_r.at[me])
    total_r[me] = total_s[...]

    bytes_of(4, others(sum_r)).wait_recv()
    stretch = half * PIECE
    for a in range(lines):
        for side in range(2):
            for c in range(half):
                where = pl.ds(a * stretch + c * PIECE, PIECE)
                own[where, :] += sum_r[a * LINE + side * half + c].astype(F32)
    fg_ref[...] = own[...].astype(BF)

    bytes_of(6, others(total_r)).wait_recv()
    for p in range(blocks):
        for t in range(per_peer):
            band, group = divmod(p * per_peer + t, groups)
            wg_ref[
                band * UNIT : (band + 1) * UNIT, group * LANES : (group + 1) * LANES
            ] = total_r[p, t].astype(F32)

    bytes_of(0, others(load_s)).wait_send()
    bytes_of(1, others(spread_r)).wait_send()
    bytes_of(2, others(serve_s)).wait_send()
    bytes_of(3, others(term_r)).wait_send()
    bytes_of(4, others(sum_s)).wait_send()
    bytes_of(5, others(grad_s)).wait_send()
    bytes_of(6, others(total_r)).wait_send()
    bytes_of(7, others(w_all)).wait_send()
    for c in range(members):
        bytes_of(8 + c, some).wait_send()


def hand_over(*refs):
    for source, dest in zip(refs[: len(refs) // 2], refs[len(refs) // 2 :]):
        dest[...] = source[...]


def per_device(
    features,
    row_target,
    tile_values,
    tile_rows,
    tile_cols,
    tile_counts,
    weight,
    layer_bias,
    out_grad,
):
    blocks = lax.axis_size("blk")
    members = lax.axis_size("rep")
    rows, cols = features.shape
    slots, tile = tile_values.shape[2:4]
    tiles = rows // tile
    bucket = 2 * rows // blocks
    assert rows == blocks * UNIT and cols == LANES and bucket % UNIT == 0
    wide = weight.shape[1]
    groups = wide // LANES
    pieces = (cols // UNIT) * groups // blocks
    half = blocks // 2
    held = blocks * PIECE
    away = PARTNERS * rows
    units = bucket // UNIT + 1
    meets = PARTNERS + 1
    slot = lax.broadcasted_iota(jnp.int32, (slots, blocks), 0)
    place = tile_rows[0].T * tiles + tile_cols[0].T
    pos = jnp.where(slot < tile_counts, place, -1)

    vmem = pl.BlockSpec(memory_space=pltpu.VMEM)
    results = pl.pallas_call(
        functools.partial(kernel, blocks, members),
        out_shape=(
            jax.ShapeDtypeStruct((rows // members, wide), BF),
            jax.ShapeDtypeStruct((cols, wide), F32),
            jax.ShapeDtypeStruct((groups, LANES), F32),
            jax.ShapeDtypeStruct((rows, cols), BF),
        ),
        in_specs=[
            vmem,
            vmem,
            pl.BlockSpec(memory_space=pltpu.SMEM),
            pl.BlockSpec(memory_space=pl.ANY),
            vmem,
            vmem,
            vmem,
        ],
        out_specs=(vmem,) * 4,
        scratch_shapes=[
            pltpu.VMEM((blocks, slots, tile, tile), BF),
            pltpu.VMEM((blocks, units, UNIT, LANES), BF),
            pltpu.VMEM((blocks, units, UNIT, LANES), BF),
            pltpu.VMEM((half, PIECE, LANES), BF),
            pltpu.VMEM((blocks, PIECE, LANES), BF),
            pltpu.VMEM((away, held), BF),
            pltpu.VMEM((held, away), BF),
            pltpu.VMEM((half, PARTNERS, PIECE, LANES), BF),
            pltpu.VMEM((PARTNERS, half, PIECE, LANES), BF),
            pltpu.VMEM((rows, meets * rows), BF),
            pltpu.VMEM((meets * rows, rows), BF),
            pltpu.VMEM((members, rows, cols), BF),
            pltpu.VMEM((members, cols, wide), BF),
            pltpu.VMEM((rows, wide), BF),
            pltpu.VMEM((members, rows // members, wide), BF),
            pltpu.VMEM((rows, cols), BF),
            pltpu.VMEM((rows, cols), F32),
            pltpu.VMEM((PARTNERS, half, PIECE, LANES), BF),
            pltpu.VMEM((half, PARTNERS, PIECE, LANES), BF),
            pltpu.VMEM((blocks, PIECE, LANES), BF),
            pltpu.VMEM((blocks, PIECE, LANES), BF),
            pltpu.VMEM((blocks, pieces + 1, UNIT, LANES), BF),
            pltpu.VMEM((blocks, pieces + 1, UNIT, LANES), BF),
            pltpu.VMEM((pieces, UNIT, LANES), BF),
            pltpu.VMEM((blocks, pieces, UNIT, LANES), BF),
            pltpu.VMEM((3 * blocks, blocks * units * UNIT), BF),
            pltpu.VMEM((rows, held), F32),
            pltpu.VMEM((UNIT, LANES), F32),
            pltpu.SemaphoreType.DMA((8 + members,)),
            pltpu.SemaphoreType.DMA((8 + members,)),
            pltpu.SemaphoreType.DMA,
        ],
        compiler_params=pltpu.CompilerParams(
            collective_id=0, has_side_effects=True, vmem_limit_bytes=58 * 2**20
        ),
    )(
        features,
        row_target.reshape(1, rows),
        pos,
        tile_values[0],
        weight,
        layer_bias.reshape(1, wide),
        out_grad,
    )
    output, weight_grad, bias_grad, feature_grad = pl.pallas_call(
        hand_over,
        out_shape=tuple(jax.ShapeDtypeStruct(r.shape, r.dtype) for r in results),
        in_specs=[vmem] * len(results),
        out_specs=(vmem,) * len(results),
    )(*results)
    return output, weight_grad, bias_grad.reshape(wide), feature_grad


def solution(mesh):
    in_specs = (
        P("blk", "rep"),
        P("blk"),
        P("blk", None, None, None, None),
        P("blk", None, None),
        P("blk", None, None),
        P("blk", None),
        P("rep", None),
        P(),
        P("blk", None),
    )
    out_specs = (P(("blk", "rep"), None), P("rep", None), P(), P("blk", "rep"))
    return jax.shard_map(
        per_device, mesh=mesh, in_specs=in_specs, out_specs=out_specs, check_vma=False
    )
```

```python
import functools
import math

import jax
import jax.numpy as jnp
from jax import lax
from jax.experimental import pallas as pl
from jax.experimental.pallas import tpu as pltpu
from jax.sharding import PartitionSpec as P

PARTNERS = 6
BF = jnp.bfloat16
F32 = jnp.float32
MESH = pl.DeviceIdType.MESH
LANES = 128
UNIT = 8
LINE = 8
LIST_AT = 64
PIECE = 16
KINDS = 4


def dot(a, b, dims=((1,), (0,))):
    return lax.dot_general(a, b, (dims, ((), ())), preferred_element_type=F32)


def iota(shape, dim):
    return lax.broadcasted_iota(jnp.int32, shape, dim).astype(F32)


def split(x, by):
    whole = jnp.floor((x + 0.5) * (1.0 / by))
    return whole, x - whole * by


def as_rows(ref):
    return ref.reshape(math.prod(ref.shape[:-1]), ref.shape[-1])


def get_rows(ref):
    return as_rows(ref)[...]


def put_rows(ref, value):
    as_rows(ref)[...] = value


def put_part(ref, first, count, value):
    size = math.prod(ref.shape[1:-1])
    start = pl.multiple_of(first * size, count * size)
    as_rows(ref)[pl.ds(start, count * size), :] = value


def step_to(kind, across):
    return (0, 1, -1, 2 - 4 * (across % 2))[kind]


def ones_where(condition):
    return jnp.where(condition, 1.0, 0.0).astype(BF)


def kernel(
    blocks,
    members,
    feat,
    target_ref,
    pos,
    tile_hbm,
    w_ref,
    bias_ref,
    og_ref,
    out_ref,
    wg_ref,
    bg_ref,
    fg_ref,
    tv,
    load_s,
    load_r,
    spread_s,
    spread_r,
    pick_t,
    pick,
    serve_s,
    serve_r,
    adj,
    adj_t,
    mixed_r,
    w_all,
    pg,
    outs,
    mg,
    own,
    term_s,
    term_r,
    sum_s,
    sum_r,
    grad_s,
    grad_r,
    total_s,
    total_r,
    offset,
    note_s,
    note_r,
    flat,
    bias_s,
    line_r,
    line_s,
    plane_r,
    send_sem,
    recv_sem,
    tile_sem,
):
    me = lax.axis_index("blk")
    member = lax.axis_index("rep")
    rows, cols = feat.shape
    slots, tile = tv.shape[1:3]
    tiles = rows // tile
    bucket = 2 * rows // blocks
    wide = w_ref.shape[1]
    loaded = blocks * bucket
    to_notes = 8 + members
    lines = blocks // LINE
    across = lax.div(me, LINE)
    along = lax.rem(me, LINE)
    half = LINE // 2
    my_class = across * half + lax.rem(along, half)
    near = lines * KINDS
    served = near * PARTNERS * PIECE
    held = blocks * PIECE
    meets = PARTNERS + 1

    load_tiles = pltpu.make_async_copy(tile_hbm, tv, tile_sem)
    load_tiles.start()
    barrier = pltpu.get_barrier_semaphore()

    def greet(d, _):
        pl.semaphore_signal(
            barrier, inc=1, device_id=(lax.rem(me + d, blocks), member), device_id_type=MESH
        )
        return 0

    lax.fori_loop(1, blocks, greet, 0)
    for d in range(1, members):
        pl.semaphore_signal(
            barrier, inc=1, device_id=(me, lax.rem(member + d, members)), device_id_type=MESH
        )

    def send_all(phase, source, dest):
        def one(d, _):
            peer = lax.rem(me + d, blocks)
            pltpu.make_async_remote_copy(
                src_ref=source(peer),
                dst_ref=dest,
                send_sem=send_sem.at[phase],
                recv_sem=recv_sem.at[phase],
                device_id=(peer, member),
                device_id_type=MESH,
            ).start()
            return 0

        lax.fori_loop(1, blocks, one, 0)

    def whom(index):
        turn, kind = split(index, KINDS)
        to = turn + across.astype(F32)
        to = jnp.where(to >= lines, to - lines, to)
        far = 2.0 - 4.0 * split(to, 2)[1]
        step = jnp.where(kind == 1, 1.0, jnp.where(kind == 2, -1.0, far))
        at = jnp.where(kind == 0, 0.0, step) + along.astype(F32)
        at = jnp.where(at < 0, at + LINE, at)
        at = jnp.where(at >= LINE, at - LINE, at)
        return to * LINE + at

    def start(phase, peer, source, dest):
        pltpu.make_async_remote_copy(
            src_ref=source,
            dst_ref=dest,
            send_sem=send_sem.at[phase],
            recv_sem=recv_sem.at[phase],
            device_id=(peer, member),
            device_id_type=MESH,
        ).start()

    def serve(turn, kind):
        to = lax.rem(across + turn, lines)
        at = lax.rem(along + step_to(kind, to) + LINE, LINE)
        return to * LINE + at, serve_s.at[turn * KINDS + kind], serve_r.at[:, my_class]

    def give_back(turn, kind):
        to = lax.rem(across + turn, lines)
        at = lax.rem(along - step_to(kind, across) + LINE, LINE)
        place = lax.rem(lines - turn, lines) * KINDS + kind
        held_class = to * half + lax.rem(at, half)
        return to * LINE + at, term_s.at[:, held_class], term_r.at[place]

    def send_members(phase, source, dest):
        for d in range(1, members):
            pltpu.make_async_remote_copy(
                src_ref=source,
                dst_ref=dest,
                send_sem=send_sem.at[phase],
                recv_sem=recv_sem.at[phase],
                device_id=(me, lax.rem(member + d, members)),
                device_id_type=MESH,
            ).start()

    def bytes_of(phase, ref):
        return pltpu.make_async_remote_copy(
            src_ref=ref,
            dst_ref=ref,
            send_sem=send_sem.at[phase],
            recv_sem=recv_sem.at[phase],
            device_id=(me, member),
            device_id_type=MESH,
        )

    def others(ref):
        return ref.at[pl.ds(0, ref.shape[0] - 1)]

    def scan(q, state):
        count, found = state
        live = (pos[0, q] >= 0) & (q != me)
        found = tuple(
            jnp.where(live & (count == k), q, f) for k, f in enumerate(found)
        )
        return count + jnp.where(live, 1, 0), found

    zero = jnp.int32(0)
    _, partners = lax.fori_loop(0, blocks, scan, (zero, (zero,) * PARTNERS))

    target = target_ref[...]
    goal, landing = split(target.astype(F32), rows)
    hits = ones_where(goal == iota((blocks, rows), 0))
    before = ones_where(iota((rows, rows), 0) < iota((rows, rows), 1))
    earlier = dot(hits, before)
    rank = jnp.sum(hits.astype(F32) * earlier, axis=0, keepdims=True)
    high, low = split(landing + 1.0, 16)
    of_rank = ones_where(rank == iota((LANES, rows), 0))
    on_lanes = ((1,), (1,))
    land_high = dot(hits * high.astype(BF), of_rank, on_lanes)
    land_low = dot(hits * low.astype(BF), of_rank, on_lanes)
    lane = lax.broadcasted_iota(jnp.int32, (blocks, LANES), 1)
    listed = jnp.zeros((blocks, LANES), jnp.int32)
    for k in range(PARTNERS):
        listed = jnp.where(lane == LIST_AT + k, partners[k], listed)
    notes = 16.0 * land_high + land_low + listed.astype(F32)
    for p in range(blocks):
        note_s[p] = notes[p : p + 1, :]
    to_slot = ones_where(goal * bucket + rank == iota((loaded, rows), 0))
    put_rows(load_s, dot(to_slot, feat[...]).astype(BF))

    pl.semaphore_wait(barrier, blocks + members - 2)
    send_all(to_notes, lambda p: note_s.at[p], note_r.at[me])
    send_all(0, lambda p: load_s.at[p], load_r.at[me])
    note_r[me] = note_s[me]
    send_members(7, w_ref, w_all.at[member])
    load_r[me] = load_s[me]
    w_all[member] = w_ref[...]
    shift = split(iota(offset.shape, 0), PIECE)[1]
    offset[...] = iota(offset.shape, 1) - shift
    fold = ones_where(iota((LANES, loaded), 0) == split(iota((LANES, loaded), 1), bucket)[1])
    bytes_of(to_notes, others(note_r)).wait_recv()
    for p in range(blocks):
        flat[p : p + 1, :] = note_r[p]
    notes = flat[...]
    high, low = split(notes, 16)
    lands = 16.0 * dot(high.astype(BF), fold) + dot(low.astype(BF), fold)
    unit = split(iota((blocks, loaded), 1), bucket)[0]
    lands = jnp.where(unit == iota((blocks, loaded), 0), lands, 0.0)
    lands = jnp.sum(lands, axis=0, keepdims=True) - 1.0
    regroup = ones_where(lands == iota((rows, loaded), 0))

    bytes_of(0, others(load_r)).wait_recv()
    got = get_rows(load_r)
    regrouped = dot(regroup, got).astype(BF)
    put_rows(spread_s, regrouped)

    def class_of(peer):
        return lax.div(peer, LINE) * half + lax.rem(lax.rem(peer, LINE), half)

    send_all(1, lambda p: spread_s.at[class_of(p)], spread_r.at[me])
    spread_r[me] = spread_s[my_class]

    lists = notes.astype(BF)
    chunk = rows

    def fill_pick_t(i, _):
        first = (i * chunk).astype(F32)
        place = split(iota((chunk, blocks), 0) + first, PARTNERS * PIECE)[0]
        for_whom = ones_where(whom(place) == iota((chunk, blocks), 1))
        nth = split(iota((chunk, LANES), 0) + first, PIECE)[0]
        nth = split(nth, PARTNERS)[1] + LIST_AT
        listed = jnp.where(nth == iota((chunk, LANES), 1), dot(for_whom, lists), 0.0)
        wanted = dot(listed.astype(BF), jnp.full((LANES, held), PIECE, BF))
        match = ones_where(wanted == offset[...])
        pick_t[pl.ds(pl.multiple_of(i * chunk, chunk), chunk), :] = match
        return 0

    lax.fori_loop(0, served // chunk, fill_pick_t, 0)
    bytes_of(1, others(spread_r)).wait_recv()
    turn_rows = KINDS * PARTNERS * PIECE

    def serve_turn(turn, _):
        part = pl.ds(pl.multiple_of(turn * turn_rows, turn_rows), turn_rows)
        pieces = dot(pick_t[part, :], get_rows(spread_r)).astype(BF)
        put_part(serve_s, turn * KINDS, KINDS, pieces)
        for kind in range(KINDS):
            start(2, *serve(turn, kind))
        return 0

    pieces = dot(pick_t[:turn_rows, :], get_rows(spread_r)).astype(BF)
    put_part(serve_s, 0, KINDS, pieces)
    for kind in range(1, KINDS):
        start(2, *serve(0, kind))
    lax.fori_loop(1, lines, serve_turn, 0)
    serve_r[:, my_class] = serve_s[0]

    load_tiles.wait()
    for k in range(meets):
        q = me if k == PARTNERS else partners[k]
        places = [pos[s, q] for s in range(slots)]
        for i in range(tiles):
            for j in range(tiles):
                chosen = zero
                live = zero
                for s in range(slots):
                    match = places[s] == i * tiles + j
                    chosen = jnp.where(match, s, chosen)
                    live = jnp.where(match, 1, live)
                values = tv[q, chosen]
                values = values * jnp.full(values.shape, live, jnp.int32).astype(F32).astype(BF)
                adj[pl.ds(i * tile, tile), pl.ds(k * rows + j * tile, tile)] = values
                adj_t[pl.ds(k * rows + j * tile, tile), pl.ds(i * tile, tile)] = values.T

    nth = split(iota((LANES, served), 1), PIECE)[0]
    nth = split(nth, PARTNERS)[1] + LIST_AT
    listed = dot(lists, ones_where(nth == iota((LANES, served), 0)))
    place = split(iota((1, served), 1), PARTNERS * PIECE)[0]
    listed = jnp.where(whom(place) == iota((blocks, served), 0), listed, 0.0)
    wanted = jnp.sum(listed, axis=0, keepdims=True)
    wanted = wanted * PIECE + split(iota((1, served), 1), PIECE)[1]
    part_rows = held // KINDS
    for c in range(KINDS):
        at = iota((part_rows, served), 0) + float(c * part_rows)
        pick[pl.ds(c * part_rows, part_rows), :] = ones_where(wanted == at)

    bytes_of(2, others(serve_s)).wait_recv()
    away = PARTNERS * rows
    share = rows // members
    for c in range(members):
        part = pl.ds(c * share, share)
        mixed = dot(adj[part, :away], get_rows(serve_r)) + dot(adj[part, away:], regrouped)
        mixed_r[member, part] = mixed.astype(BF)
        send_members(8 + c, mixed_r.at[member, part], mixed_r.at[member, part])
    bytes_of(7, others(w_all)).wait_recv()
    some = mixed_r.at[pl.ds(0, members - 1), pl.ds(0, share)]

    bias_part = jnp.zeros((1, wide), F32)
    for c in range(members):
        part = pl.ds(c * share, share)
        bytes_of(8 + c, some).wait_recv()
        pre = dot(mixed_r[0, part], w_all[0])
        for r in range(1, members):
            pre = pre + dot(mixed_r[r, part], w_all[r])
        pre = pre + bias_ref[...]
        sigma = jax.nn.sigmoid(pre)
        outs[c] = (pre * sigma).astype(BF)
        grad = og_ref[part, :].astype(F32) * sigma * (1.0 + pre * (1.0 - sigma))
        grad = grad.astype(BF)
        pg[part, :] = grad
        bias_part = bias_part + jnp.sum(grad.astype(F32), axis=0, keepdims=True)
        mg[part, :] = dot(grad, w_ref[...], on_lanes).astype(BF)
    out_ref[...] = outs[member]

    put_rows(term_s, dot(adj_t[:away], mg[...]).astype(BF))
    for kind in range(1, KINDS):
        start(3, *give_back(0, kind))

    def give_turn(turn, _):
        for kind in range(KINDS):
            start(3, *give_back(turn, kind))
        return 0

    lax.fori_loop(1, lines, give_turn, 0)
    term_r[0] = term_s[:, my_class]
    own[...] = dot(adj_t[away:], mg[...])

    groups = wide // LANES
    for g in range(groups):
        bias_s[g : g + 1, :] = bias_part[:, g * LANES : (g + 1) * LANES]
    for d in range(1, LINE):
        peer = across * LINE + lax.rem(along + d, LINE)
        start(to_notes + 1, peer, bias_s, line_r.at[along])
    line_r[along] = bias_s[...]

    weight_part = dot(mixed_r[member].T, pg[...])
    per_peer = (cols // UNIT) * groups // blocks
    for p in range(blocks):
        for t in range(per_peer):
            band, group = divmod(p * per_peer + t, groups)
            grad_s[p, t] = weight_part[
                band * UNIT : (band + 1) * UNIT, group * LANES : (group + 1) * LANES
            ].astype(BF)
    send_all(5, lambda p: grad_s.at[p], grad_r.at[me])
    grad_r[me] = grad_s[me]

    bytes_of(to_notes + 1, others(line_r)).wait_recv()
    line_s[...] = jnp.sum(line_r[...], axis=0)

    def pass_on(d, _):
        peer = lax.rem(across + d, lines) * LINE + along
        start(to_notes + 2, peer, line_s, plane_r.at[across])
        return 0

    lax.fori_loop(1, lines, pass_on, 0)
    plane_r[across] = line_s[...]

    bytes_of(3, others(term_r)).wait_recv()
    some_lines = max(1, lines // 4)
    together = some_lines * LINE
    for turn in range(lines // some_lines):
        line = lax.rem(lax.div(across, some_lines) * some_lines + turn * some_lines, lines)
        part = pl.ds(pl.multiple_of(line * LINE * PIECE, together * PIECE), together * PIECE)
        sums = dot(pick[part, :], get_rows(term_r)).astype(BF)
        put_part(sum_s, line * LINE, together, sums)

        def hand_back(d, _, line=line):
            peer = line * LINE + lax.rem(me + d, together)
            start(4, peer, sum_s.at[peer], sum_r.at[me])
            return 0

        lax.fori_loop(1 if turn == 0 else 0, together, hand_back, 0)
    sum_r[me] = sum_s[me]

    bytes_of(5, others(grad_r)).wait_recv()
    total = grad_r[0].astype(F32)
    for p in range(1, blocks):
        total = total + grad_r[p].astype(F32)
    total_s[...] = total.astype(BF)
    send_all(6, lambda p: total_s, total_r.at[me])
    total_r[me] = total_s[...]

    bytes_of(to_notes + 2, others(plane_r)).wait_recv()
    bg_ref[...] = jnp.sum(plane_r[...], axis=0)

    bytes_of(4, others(sum_r)).wait_recv()
    stretch = half * PIECE
    for a in range(lines):
        for side in range(2):
            for c in range(half):
                where = pl.ds(a * stretch + c * PIECE, PIECE)
                own[where, :] += sum_r[a * LINE + side * half + c].astype(F32)
    fg_ref[...] = own[...].astype(BF)

    bytes_of(6, others(total_r)).wait_recv()
    for p in range(blocks):
        for t in range(per_peer):
            band, group = divmod(p * per_peer + t, groups)
            wg_ref[
                band * UNIT : (band + 1) * UNIT, group * LANES : (group + 1) * LANES
            ] = total_r[p, t].astype(F32)

    bytes_of(0, others(load_s)).wait_send()
    bytes_of(1, others(spread_r)).wait_send()
    bytes_of(2, others(serve_s)).wait_send()
    bytes_of(3, others(term_r)).wait_send()
    bytes_of(4, others(sum_s)).wait_send()
    bytes_of(5, others(grad_s)).wait_send()
    bytes_of(6, others(total_r)).wait_send()
    bytes_of(7, others(w_all)).wait_send()
    for c in range(members):
        bytes_of(8 + c, some).wait_send()
    bytes_of(to_notes, others(note_r)).wait_send()
    bytes_of(to_notes + 1, others(line_r)).wait_send()
    bytes_of(to_notes + 2, others(plane_r)).wait_send()


def hand_over(*refs):
    for source, dest in zip(refs[: len(refs) // 2], refs[len(refs) // 2 :]):
        dest[...] = source[...]


def per_device(
    features,
    row_target,
    tile_values,
    tile_rows,
    tile_cols,
    tile_counts,
    weight,
    layer_bias,
    out_grad,
):
    blocks = lax.axis_size("blk")
    members = lax.axis_size("rep")
    rows, cols = features.shape
    slots, tile = tile_values.shape[2:4]
    tiles = rows // tile
    bucket = 2 * rows // blocks
    assert rows == blocks * UNIT and cols == LANES and bucket == PIECE
    wide = weight.shape[1]
    groups = wide // LANES
    pieces = (cols // UNIT) * groups // blocks
    half = blocks // 2
    held = blocks * PIECE
    away = PARTNERS * rows
    meets = PARTNERS + 1
    slot = lax.broadcasted_iota(jnp.int32, (slots, blocks), 0)
    place = tile_rows[0].T * tiles + tile_cols[0].T
    pos = jnp.where(slot < tile_counts, place, -1)

    vmem = pl.BlockSpec(memory_space=pltpu.VMEM)
    results = pl.pallas_call(
        functools.partial(kernel, blocks, members),
        out_shape=(
            jax.ShapeDtypeStruct((rows // members, wide), BF),
            jax.ShapeDtypeStruct((cols, wide), F32),
            jax.ShapeDtypeStruct((groups, LANES), F32),
            jax.ShapeDtypeStruct((rows, cols), BF),
        ),
        in_specs=[
            vmem,
            vmem,
            pl.BlockSpec(memory_space=pltpu.SMEM),
            pl.BlockSpec(memory_space=pl.ANY),
            vmem,
            vmem,
            vmem,
        ],
        out_specs=(vmem,) * 4,
        scratch_shapes=[
            pltpu.VMEM((blocks, slots, tile, tile), BF),
            pltpu.VMEM((blocks, bucket, LANES), BF),
            pltpu.VMEM((blocks, bucket, LANES), BF),
            pltpu.VMEM((half, PIECE, LANES), BF),
            pltpu.VMEM((blocks, PIECE, LANES), BF),
            pltpu.VMEM((away, held), BF),
            pltpu.VMEM((held, away), BF),
            pltpu.VMEM((half, PARTNERS, PIECE, LANES), BF),
            pltpu.VMEM((PARTNERS, half, PIECE, LANES), BF),
            pltpu.VMEM((rows, meets * rows), BF),
            pltpu.VMEM((meets * rows, rows), BF),
            pltpu.VMEM((members, rows, cols), BF),
            pltpu.VMEM((members, cols, wide), BF),
            pltpu.VMEM((rows, wide), BF),
            pltpu.VMEM((members, rows // members, wide), BF),
            pltpu.VMEM((rows, cols), BF),
            pltpu.VMEM((rows, cols), F32),
            pltpu.VMEM((PARTNERS, half, PIECE, LANES), BF),
            pltpu.VMEM((half, PARTNERS, PIECE, LANES), BF),
            pltpu.VMEM((blocks, PIECE, LANES), BF),
            pltpu.VMEM((blocks, PIECE, LANES), BF),
            pltpu.VMEM((blocks, pieces, UNIT, LANES), BF),
            pltpu.VMEM((blocks, pieces, UNIT, LANES), BF),
            pltpu.VMEM((pieces, UNIT, LANES), BF),
            pltpu.VMEM((blocks, pieces, UNIT, LANES), BF),
            pltpu.VMEM((rows, held), F32),
            pltpu.VMEM((blocks, 1, LANES), F32),
            pltpu.VMEM((blocks, 1, LANES), F32),
            pltpu.VMEM((blocks, LANES), F32),
            pltpu.VMEM((groups, LANES), F32),
            pltpu.VMEM((LINE, groups, LANES), F32),
            pltpu.VMEM((groups, LANES), F32),
            pltpu.VMEM((blocks // LINE, groups, LANES), F32),
            pltpu.SemaphoreType.DMA((11 + members,)),
            pltpu.SemaphoreType.DMA((11 + members,)),
            pltpu.SemaphoreType.DMA,
        ],
        compiler_params=pltpu.CompilerParams(
            collective_id=0, has_side_effects=True, vmem_limit_bytes=58 * 2**20
        ),
    )(
        features,
        row_target.reshape(1, rows),
        pos,
        tile_values[0],
        weight,
        layer_bias.reshape(1, wide),
        out_grad,
    )
    output, weight_grad, bias_grad, feature_grad = pl.pallas_call(
        hand_over,
        out_shape=tuple(jax.ShapeDtypeStruct(r.shape, r.dtype) for r in results),
        in_specs=[vmem] * len(results),
        out_specs=(vmem,) * len(results),
    )(*results)
    return output, weight_grad, bias_grad.reshape(wide), feature_grad


def solution(mesh):
    in_specs = (
        P("blk", "rep"),
        P("blk"),
        P("blk", None, None, None, None),
        P("blk", None, None),
        P("blk", None, None),
        P("blk", None),
        P("rep", None),
        P(),
        P("blk", None),
    )
    out_specs = (P(("blk", "rep"), None), P("rep", None), P(), P("blk", "rep"))
    return jax.shard_map(
        per_device, mesh=mesh, in_specs=in_specs, out_specs=out_specs, check_vma=False
    )
```

```python
import functools
import math

import jax
import jax.numpy as jnp
from jax import lax
from jax.experimental import pallas as pl
from jax.experimental.pallas import tpu as pltpu
from jax.sharding import PartitionSpec as P

PARTNERS = 6
BF = jnp.bfloat16
F32 = jnp.float32
MESH = pl.DeviceIdType.MESH
LANES = 128
UNIT = 8
LINE = 8
LIST_AT = 64
PIECE = 16
KINDS = 4


def dot(a, b, dims=((1,), (0,))):
    return lax.dot_general(a, b, (dims, ((), ())), preferred_element_type=F32)


def iota(shape, dim):
    return lax.broadcasted_iota(jnp.int32, shape, dim).astype(F32)


def split(x, by):
    whole = jnp.floor((x + 0.5) * (1.0 / by))
    return whole, x - whole * by


def as_rows(ref):
    return ref.reshape(math.prod(ref.shape[:-1]), ref.shape[-1])


def get_rows(ref):
    return as_rows(ref)[...]


def put_rows(ref, value):
    as_rows(ref)[...] = value


def put_part(ref, first, count, value):
    size = math.prod(ref.shape[1:-1])
    start = pl.multiple_of(first * size, count * size)
    as_rows(ref)[pl.ds(start, count * size), :] = value


def step_to(kind, across):
    return (0, 1, -1, 2 - 4 * (across % 2))[kind]


def ones_where(condition):
    return jnp.where(condition, 1.0, 0.0).astype(BF)


def kernel(
    blocks,
    members,
    feat,
    target_ref,
    tile_row,
    tile_col,
    counts,
    tile_hbm,
    w_ref,
    bias_ref,
    og_ref,
    out_ref,
    wg_ref,
    bg_ref,
    fg_ref,
    tv,
    load_s,
    load_r,
    spread_s,
    spread_r,
    pick_t,
    pick,
    serve_s,
    serve_r,
    adj,
    adj_t,
    mixed_r,
    w_all,
    pg,
    outs,
    mg,
    own,
    term_s,
    term_r,
    sum_s,
    sum_r,
    grad_s,
    grad_r,
    total_s,
    total_r,
    offset,
    note_s,
    note_r,
    flat,
    bias_s,
    line_r,
    line_s,
    plane_r,
    send_sem,
    recv_sem,
    tile_sem,
):
    me = lax.axis_index("blk")
    member = lax.axis_index("rep")
    rows, cols = feat.shape
    slots, tile = tv.shape[1:3]
    tiles = rows // tile
    bucket = 2 * rows // blocks
    wide = w_ref.shape[1]
    loaded = blocks * bucket
    to_notes = 8 + members
    lines = blocks // LINE
    across = lax.div(me, LINE)
    along = lax.rem(me, LINE)
    half = LINE // 2
    my_class = across * half + lax.rem(along, half)
    near = lines * KINDS
    served = near * PARTNERS * PIECE
    held = blocks * PIECE
    meets = PARTNERS + 1

    load_tiles = pltpu.make_async_copy(tile_hbm, tv, tile_sem)
    load_tiles.start()
    barrier = pltpu.get_barrier_semaphore()

    def greet(d, _):
        pl.semaphore_signal(
            barrier, inc=1, device_id=(lax.rem(me + d, blocks), member), device_id_type=MESH
        )
        return 0

    lax.fori_loop(1, blocks, greet, 0)
    for d in range(1, members):
        pl.semaphore_signal(
            barrier, inc=1, device_id=(me, lax.rem(member + d, members)), device_id_type=MESH
        )

    def send_all(phase, source, dest):
        def one(d, _):
            peer = lax.rem(me + d, blocks)
            pltpu.make_async_remote_copy(
                src_ref=source(peer),
                dst_ref=dest,
                send_sem=send_sem.at[phase],
                recv_sem=recv_sem.at[phase],
                device_id=(peer, member),
                device_id_type=MESH,
            ).start()
            return 0

        lax.fori_loop(1, blocks, one, 0)

    def whom(index):
        turn, kind = split(index, KINDS)
        to = turn + across.astype(F32)
        to = jnp.where(to >= lines, to - lines, to)
        far = 2.0 - 4.0 * split(to, 2)[1]
        step = jnp.where(kind == 1, 1.0, jnp.where(kind == 2, -1.0, far))
        at = jnp.where(kind == 0, 0.0, step) + along.astype(F32)
        at = jnp.where(at < 0, at + LINE, at)
        at = jnp.where(at >= LINE, at - LINE, at)
        return to * LINE + at

    def start(phase, peer, source, dest):
        pltpu.make_async_remote_copy(
            src_ref=source,
            dst_ref=dest,
            send_sem=send_sem.at[phase],
            recv_sem=recv_sem.at[phase],
            device_id=(peer, member),
            device_id_type=MESH,
        ).start()

    def serve(turn, kind):
        to = lax.rem(across + turn, lines)
        at = lax.rem(along + step_to(kind, to) + LINE, LINE)
        return to * LINE + at, serve_s.at[turn * KINDS + kind], serve_r.at[:, my_class]

    def give_back(turn, kind):
        to = lax.rem(across + turn, lines)
        at = lax.rem(along - step_to(kind, across) + LINE, LINE)
        place = lax.rem(lines - turn, lines) * KINDS + kind
        held_class = to * half + lax.rem(at, half)
        return to * LINE + at, term_s.at[:, held_class], term_r.at[place]

    def send_members(phase, source, dest):
        for d in range(1, members):
            pltpu.make_async_remote_copy(
                src_ref=source,
                dst_ref=dest,
                send_sem=send_sem.at[phase],
                recv_sem=recv_sem.at[phase],
                device_id=(me, lax.rem(member + d, members)),
                device_id_type=MESH,
            ).start()

    def bytes_of(phase, ref):
        return pltpu.make_async_remote_copy(
            src_ref=ref,
            dst_ref=ref,
            send_sem=send_sem.at[phase],
            recv_sem=recv_sem.at[phase],
            device_id=(me, member),
            device_id_type=MESH,
        )

    def others(ref):
        return ref.at[pl.ds(0, ref.shape[0] - 1)]

    def scan(q, state):
        count, found = state
        live = (counts[0, q] > 0) & (q != me)
        found = tuple(
            jnp.where(live & (count == k), q, f) for k, f in enumerate(found)
        )
        return count + jnp.where(live, 1, 0), found

    zero = jnp.int32(0)
    _, partners = lax.fori_loop(0, blocks, scan, (zero, (zero,) * PARTNERS))

    target = target_ref[...]
    goal, landing = split(target.astype(F32), rows)
    hits = ones_where(goal == iota((blocks, rows), 0))
    before = ones_where(iota((rows, rows), 0) < iota((rows, rows), 1))
    earlier = dot(hits, before)
    rank = jnp.sum(hits.astype(F32) * earlier, axis=0, keepdims=True)
    high, low = split(landing + 1.0, 16)
    of_rank = ones_where(rank == iota((LANES, rows), 0))
    on_lanes = ((1,), (1,))
    land_high = dot(hits * high.astype(BF), of_rank, on_lanes)
    land_low = dot(hits * low.astype(BF), of_rank, on_lanes)
    lane = lax.broadcasted_iota(jnp.int32, (blocks, LANES), 1)
    listed = jnp.zeros((blocks, LANES), jnp.int32)
    for k in range(PARTNERS):
        listed = jnp.where(lane == LIST_AT + k, partners[k], listed)
    notes = 16.0 * land_high + land_low + listed.astype(F32)
    for p in range(blocks):
        note_s[p] = notes[p : p + 1, :]
    to_slot = ones_where(goal * bucket + rank == iota((loaded, rows), 0))
    put_rows(load_s, dot(to_slot, feat[...]).astype(BF))

    pl.semaphore_wait(barrier, blocks + members - 2)
    send_all(to_notes, lambda p: note_s.at[p], note_r.at[me])
    send_all(0, lambda p: load_s.at[p], load_r.at[me])
    note_r[me] = note_s[me]
    send_members(7, w_ref, w_all.at[member])
    load_r[me] = load_s[me]
    w_all[member] = w_ref[...]
    shift = split(iota(offset.shape, 0), PIECE)[1]
    offset[...] = iota(offset.shape, 1) - shift
    fold = ones_where(iota((LANES, loaded), 0) == split(iota((LANES, loaded), 1), bucket)[1])
    bytes_of(to_notes, others(note_r)).wait_recv()
    for p in range(blocks):
        flat[p : p + 1, :] = note_r[p]
    notes = flat[...]
    high, low = split(notes, 16)
    lands = 16.0 * dot(high.astype(BF), fold) + dot(low.astype(BF), fold)
    unit = split(iota((blocks, loaded), 1), bucket)[0]
    lands = jnp.where(unit == iota((blocks, loaded), 0), lands, 0.0)
    lands = jnp.sum(lands, axis=0, keepdims=True) - 1.0
    regroup = ones_where(lands == iota((rows, loaded), 0))

    bytes_of(0, others(load_r)).wait_recv()
    got = get_rows(load_r)
    regrouped = dot(regroup, got).astype(BF)
    put_rows(spread_s, regrouped)

    def class_of(peer):
        return lax.div(peer, LINE) * half + lax.rem(lax.rem(peer, LINE), half)

    send_all(1, lambda p: spread_s.at[class_of(p)], spread_r.at[me])
    spread_r[me] = spread_s[my_class]

    lists = notes.astype(BF)
    chunk = rows

    def fill_pick_t(i, _):
        first = (i * chunk).astype(F32)
        place = split(iota((chunk, blocks), 0) + first, PARTNERS * PIECE)[0]
        for_whom = ones_where(whom(place) == iota((chunk, blocks), 1))
        nth = split(iota((chunk, LANES), 0) + first, PIECE)[0]
        nth = split(nth, PARTNERS)[1] + LIST_AT
        listed = jnp.where(nth == iota((chunk, LANES), 1), dot(for_whom, lists), 0.0)
        wanted = dot(listed.astype(BF), jnp.full((LANES, held), PIECE, BF))
        match = ones_where(wanted == offset[...])
        pick_t[pl.ds(pl.multiple_of(i * chunk, chunk), chunk), :] = match
        return 0

    lax.fori_loop(0, served // chunk, fill_pick_t, 0)
    bytes_of(1, others(spread_r)).wait_recv()
    turn_rows = KINDS * PARTNERS * PIECE

    def serve_turn(turn, _):
        part = pl.ds(pl.multiple_of(turn * turn_rows, turn_rows), turn_rows)
        pieces = dot(pick_t[part, :], get_rows(spread_r)).astype(BF)
        put_part(serve_s, turn * KINDS, KINDS, pieces)
        for kind in range(KINDS):
            start(2, *serve(turn, kind))
        return 0

    pieces = dot(pick_t[:turn_rows, :], get_rows(spread_r)).astype(BF)
    put_part(serve_s, 0, KINDS, pieces)
    for kind in range(1, KINDS):
        start(2, *serve(0, kind))
    lax.fori_loop(1, lines, serve_turn, 0)
    serve_r[:, my_class] = serve_s[0]

    load_tiles.wait()
    for k in range(meets):
        q = me if k == PARTNERS else partners[k]
        places = [
            jnp.where(s < counts[0, q], tile_row[s, q] * tiles + tile_col[s, q], -1)
            for s in range(slots)
        ]
        for i in range(tiles):
            for j in range(tiles):
                chosen = zero
                live = zero
                for s in range(slots):
                    match = places[s] == i * tiles + j
                    chosen = jnp.where(match, s, chosen)
                    live = jnp.where(match, 1, live)
                values = tv[q, chosen]
                values = values * jnp.full(values.shape, live, jnp.int32).astype(F32).astype(BF)
                adj[pl.ds(i * tile, tile), pl.ds(k * rows + j * tile, tile)] = values
                adj_t[pl.ds(k * rows + j * tile, tile), pl.ds(i * tile, tile)] = values.T

    nth = split(iota((LANES, served), 1), PIECE)[0]
    nth = split(nth, PARTNERS)[1] + LIST_AT
    listed = dot(lists, ones_where(nth == iota((LANES, served), 0)))
    place = split(iota((1, served), 1), PARTNERS * PIECE)[0]
    listed = jnp.where(whom(place) == iota((blocks, served), 0), listed, 0.0)
    wanted = jnp.sum(listed, axis=0, keepdims=True)
    wanted = wanted * PIECE + split(iota((1, served), 1), PIECE)[1]
    part_rows = held // KINDS
    for c in range(KINDS):
        at = iota((part_rows, served), 0) + float(c * part_rows)
        pick[pl.ds(c * part_rows, part_rows), :] = ones_where(wanted == at)

    bytes_of(2, others(serve_s)).wait_recv()
    away = PARTNERS * rows
    share = rows // members
    for c in range(members):
        part = pl.ds(c * share, share)
        mixed = dot(adj[part, :away], get_rows(serve_r)) + dot(adj[part, away:], regrouped)
        mixed_r[member, part] = mixed.astype(BF)
        send_members(8 + c, mixed_r.at[member, part], mixed_r.at[member, part])
    bytes_of(7, others(w_all)).wait_recv()
    some = mixed_r.at[pl.ds(0, members - 1), pl.ds(0, share)]

    bias_part = jnp.zeros((1, wide), F32)
    for c in range(members):
        part = pl.ds(c * share, share)
        bytes_of(8 + c, some).wait_recv()
        pre = dot(mixed_r[0, part], w_all[0])
        for r in range(1, members):
            pre = pre + dot(mixed_r[r, part], w_all[r])
        pre = pre + bias_ref[...]
        sigma = jax.nn.sigmoid(pre)
        outs[c] = (pre * sigma).astype(BF)
        grad = og_ref[part, :].astype(F32) * sigma * (1.0 + pre * (1.0 - sigma))
        grad = grad.astype(BF)
        pg[part, :] = grad
        bias_part = bias_part + jnp.sum(grad.astype(F32), axis=0, keepdims=True)
        mg[part, :] = dot(grad, w_ref[...], on_lanes).astype(BF)
    out_ref[...] = outs[member]

    put_rows(term_s, dot(adj_t[:away], mg[...]).astype(BF))
    for kind in range(1, KINDS):
        start(3, *give_back(0, kind))

    def give_turn(turn, _):
        for kind in range(KINDS):
            start(3, *give_back(turn, kind))
        return 0

    lax.fori_loop(1, lines, give_turn, 0)
    term_r[0] = term_s[:, my_class]
    own[...] = dot(adj_t[away:], mg[...])

    groups = wide // LANES
    for g in range(groups):
        bias_s[g : g + 1, :] = bias_part[:, g * LANES : (g + 1) * LANES]
    for d in range(1, LINE):
        peer = across * LINE + lax.rem(along + d, LINE)
        start(to_notes + 1, peer, bias_s, line_r.at[along])
    line_r[along] = bias_s[...]

    weight_part = dot(mixed_r[member].T, pg[...])
    per_peer = (cols // UNIT) * groups // blocks
    for p in range(blocks):
        for t in range(per_peer):
            band, group = divmod(p * per_peer + t, groups)
            grad_s[p, t] = weight_part[
                band * UNIT : (band + 1) * UNIT, group * LANES : (group + 1) * LANES
            ].astype(BF)
    send_all(5, lambda p: grad_s.at[p], grad_r.at[me])
    grad_r[me] = grad_s[me]

    bytes_of(to_notes + 1, others(line_r)).wait_recv()
    line_s[...] = jnp.sum(line_r[...], axis=0)

    def pass_on(d, _):
        peer = lax.rem(across + d, lines) * LINE + along
        start(to_notes + 2, peer, line_s, plane_r.at[across])
        return 0

    lax.fori_loop(1, lines, pass_on, 0)
    plane_r[across] = line_s[...]

    bytes_of(5, others(grad_r)).wait_recv()
    total = grad_r[0].astype(F32)
    for p in range(1, blocks):
        total = total + grad_r[p].astype(F32)
    total_s[...] = total.astype(BF)
    send_all(6, lambda p: total_s, total_r.at[me])
    total_r[me] = total_s[...]

    bytes_of(3, others(term_r)).wait_recv()
    some_lines = max(1, lines // 4)
    together = some_lines * LINE
    for turn in range(lines // some_lines):
        line = lax.rem(lax.div(across, some_lines) * some_lines + turn * some_lines, lines)
        part = pl.ds(pl.multiple_of(line * LINE * PIECE, together * PIECE), together * PIECE)
        sums = dot(pick[part, :], get_rows(term_r)).astype(BF)
        put_part(sum_s, line * LINE, together, sums)

        def hand_back(d, _, line=line):
            peer = line * LINE + lax.rem(me + d, together)
            start(4, peer, sum_s.at[peer], sum_r.at[me])
            return 0

        lax.fori_loop(1 if turn == 0 else 0, together, hand_back, 0)
    sum_r[me] = sum_s[me]

    bytes_of(to_notes + 2, others(plane_r)).wait_recv()
    bg_ref[...] = jnp.sum(plane_r[...], axis=0)

    bytes_of(6, others(total_r)).wait_recv()
    for p in range(blocks):
        for t in range(per_peer):
            band, group = divmod(p * per_peer + t, groups)
            wg_ref[
                band * UNIT : (band + 1) * UNIT, group * LANES : (group + 1) * LANES
            ] = total_r[p, t].astype(F32)

    bytes_of(4, others(sum_r)).wait_recv()
    stretch = half * PIECE
    for a in range(lines):
        for side in range(2):
            for c in range(half):
                where = pl.ds(a * stretch + c * PIECE, PIECE)
                own[where, :] += sum_r[a * LINE + side * half + c].astype(F32)
    fg_ref[...] = own[...].astype(BF)

    bytes_of(0, others(load_s)).wait_send()
    bytes_of(1, others(spread_r)).wait_send()
    bytes_of(2, others(serve_s)).wait_send()
    bytes_of(3, others(term_r)).wait_send()
    bytes_of(4, others(sum_s)).wait_send()
    bytes_of(5, others(grad_s)).wait_send()
    bytes_of(6, others(total_r)).wait_send()
    bytes_of(7, others(w_all)).wait_send()
    for c in range(members):
        bytes_of(8 + c, some).wait_send()
    bytes_of(to_notes, others(note_r)).wait_send()
    bytes_of(to_notes + 1, others(line_r)).wait_send()
    bytes_of(to_notes + 2, others(plane_r)).wait_send()


def hand_over(*refs):
    for source, dest in zip(refs[: len(refs) // 2], refs[len(refs) // 2 :]):
        dest[...] = source[...]


def per_device(
    features,
    row_target,
    tile_values,
    tile_rows,
    tile_cols,
    tile_counts,
    weight,
    layer_bias,
    out_grad,
):
    blocks = lax.axis_size("blk")
    members = lax.axis_size("rep")
    rows, cols = features.shape
    slots, tile = tile_values.shape[2:4]
    bucket = 2 * rows // blocks
    assert rows == blocks * UNIT and cols == LANES and bucket == PIECE
    wide = weight.shape[1]
    groups = wide // LANES
    pieces = (cols // UNIT) * groups // blocks
    half = blocks // 2
    held = blocks * PIECE
    away = PARTNERS * rows
    meets = PARTNERS + 1
    smem = pl.BlockSpec(memory_space=pltpu.SMEM)
    vmem = pl.BlockSpec(memory_space=pltpu.VMEM)
    results = pl.pallas_call(
        functools.partial(kernel, blocks, members),
        out_shape=(
            jax.ShapeDtypeStruct((rows // members, wide), BF),
            jax.ShapeDtypeStruct((cols, wide), F32),
            jax.ShapeDtypeStruct((groups, LANES), F32),
            jax.ShapeDtypeStruct((rows, cols), BF),
        ),
        in_specs=[
            vmem,
            vmem,
            smem,
            smem,
            smem,
            pl.BlockSpec(memory_space=pl.ANY),
            vmem,
            vmem,
            vmem,
        ],
        out_specs=(vmem,) * 4,
        scratch_shapes=[
            pltpu.VMEM((blocks, slots, tile, tile), BF),
            pltpu.VMEM((blocks, bucket, LANES), BF),
            pltpu.VMEM((blocks, bucket, LANES), BF),
            pltpu.VMEM((half, PIECE, LANES), BF),
            pltpu.VMEM((blocks, PIECE, LANES), BF),
            pltpu.VMEM((away, held), BF),
            pltpu.VMEM((held, away), BF),
            pltpu.VMEM((half, PARTNERS, PIECE, LANES), BF),
            pltpu.VMEM((PARTNERS, half, PIECE, LANES), BF),
            pltpu.VMEM((rows, meets * rows), BF),
            pltpu.VMEM((meets * rows, rows), BF),
            pltpu.VMEM((members, rows, cols), BF),
            pltpu.VMEM((members, cols, wide), BF),
            pltpu.VMEM((rows, wide), BF),
            pltpu.VMEM((members, rows // members, wide), BF),
            pltpu.VMEM((rows, cols), BF),
            pltpu.VMEM((rows, cols), F32),
            pltpu.VMEM((PARTNERS, half, PIECE, LANES), BF),
            pltpu.VMEM((half, PARTNERS, PIECE, LANES), BF),
            pltpu.VMEM((blocks, PIECE, LANES), BF),
            pltpu.VMEM((blocks, PIECE, LANES), BF),
            pltpu.VMEM((blocks, pieces, UNIT, LANES), BF),
            pltpu.VMEM((blocks, pieces, UNIT, LANES), BF),
            pltpu.VMEM((pieces, UNIT, LANES), BF),
            pltpu.VMEM((blocks, pieces, UNIT, LANES), BF),
            pltpu.VMEM((rows, held), F32),
            pltpu.VMEM((blocks, 1, LANES), F32),
            pltpu.VMEM((blocks, 1, LANES), F32),
            pltpu.VMEM((blocks, LANES), F32),
            pltpu.VMEM((groups, LANES), F32),
            pltpu.VMEM((LINE, groups, LANES), F32),
            pltpu.VMEM((groups, LANES), F32),
            pltpu.VMEM((blocks // LINE, groups, LANES), F32),
            pltpu.SemaphoreType.DMA((11 + members,)),
            pltpu.SemaphoreType.DMA((11 + members,)),
            pltpu.SemaphoreType.DMA,
        ],
        compiler_params=pltpu.CompilerParams(
            collective_id=0, has_side_effects=True, vmem_limit_bytes=58 * 2**20
        ),
    )(
        features,
        row_target.reshape(1, rows),
        tile_rows[0].T,
        tile_cols[0].T,
        tile_counts,
        tile_values[0],
        weight,
        layer_bias.reshape(1, wide),
        out_grad,
    )
    output, weight_grad, bias_grad, feature_grad = pl.pallas_call(
        hand_over,
        out_shape=tuple(jax.ShapeDtypeStruct(r.shape, r.dtype) for r in results),
        in_specs=[vmem] * len(results),
        out_specs=(vmem,) * len(results),
    )(*results)
    return output, weight_grad, bias_grad.reshape(wide), feature_grad


def solution(mesh):
    in_specs = (
        P("blk", "rep"),
        P("blk"),
        P("blk", None, None, None, None),
        P("blk", None, None),
        P("blk", None, None),
        P("blk", None),
        P("rep", None),
        P(),
        P("blk", None),
    )
    out_specs = (P(("blk", "rep"), None), P("rep", None), P(), P("blk", "rep"))
    return jax.shard_map(
        per_device, mesh=mesh, in_specs=in_specs, out_specs=out_specs, check_vma=False
    )
```

```python
import functools
import math

import jax
import jax.numpy as jnp
from jax import lax
from jax.experimental import pallas as pl
from jax.experimental.pallas import tpu as pltpu
from jax.sharding import PartitionSpec as P

PARTNERS = 6
BF = jnp.bfloat16
F32 = jnp.float32
MESH = pl.DeviceIdType.MESH
LANES = 128
UNIT = 8
LINE = 8
LIST_AT = 64
PIECE = 16
KINDS = 4


def dot(a, b, dims=((1,), (0,))):
    return lax.dot_general(a, b, (dims, ((), ())), preferred_element_type=F32)


def iota(shape, dim):
    return lax.broadcasted_iota(jnp.int32, shape, dim).astype(F32)


def split(x, by):
    whole = jnp.floor((x + 0.5) * (1.0 / by))
    return whole, x - whole * by


def as_rows(ref):
    return ref.reshape(math.prod(ref.shape[:-1]), ref.shape[-1])


def get_rows(ref):
    return as_rows(ref)[...]


def put_rows(ref, value):
    as_rows(ref)[...] = value


def put_part(ref, first, count, value):
    size = math.prod(ref.shape[1:-1])
    start = pl.multiple_of(first * size, count * size)
    as_rows(ref)[pl.ds(start, count * size), :] = value


def step_to(kind, across):
    return (0, 1, -1, 2 - 4 * (across % 2))[kind]


def ones_where(condition):
    return jnp.where(condition, 1.0, 0.0).astype(BF)


def kernel(
    blocks,
    members,
    feat,
    target_ref,
    tile_row,
    tile_col,
    counts,
    tile_hbm,
    w_ref,
    bias_ref,
    og_ref,
    out_ref,
    wg_ref,
    bg_ref,
    fg_ref,
    tv,
    load_s,
    load_r,
    spread_s,
    spread_r,
    pick_t,
    pick,
    serve_s,
    serve_r,
    adj,
    adj_t,
    mixed_r,
    w_all,
    pg,
    outs,
    mg,
    own,
    term_s,
    term_r,
    sum_s,
    sum_r,
    grad_s,
    grad_r,
    total_s,
    total_r,
    offset,
    note_s,
    note_r,
    flat,
    bias_s,
    line_r,
    line_s,
    plane_r,
    send_sem,
    recv_sem,
    tile_sem,
):
    me = lax.axis_index("blk")
    member = lax.axis_index("rep")
    rows, cols = feat.shape
    slots, tile = tv.shape[1:3]
    tiles = rows // tile
    bucket = 2 * rows // blocks
    wide = w_ref.shape[1]
    loaded = blocks * bucket
    to_notes = 8 + members
    lines = blocks // LINE
    across = lax.div(me, LINE)
    along = lax.rem(me, LINE)
    half = LINE // 2
    my_class = across * half + lax.rem(along, half)
    near = lines * KINDS
    served = near * PARTNERS * PIECE
    held = blocks * PIECE
    meets = PARTNERS + 1

    load_tiles = pltpu.make_async_copy(tile_hbm, tv, tile_sem)
    load_tiles.start()
    barrier = pltpu.get_barrier_semaphore()

    def greet(d, _):
        pl.semaphore_signal(
            barrier, inc=1, device_id=(lax.rem(me + d, blocks), member), device_id_type=MESH
        )
        return 0

    lax.fori_loop(1, blocks, greet, 0)
    for d in range(1, members):
        pl.semaphore_signal(
            barrier, inc=1, device_id=(me, lax.rem(member + d, members)), device_id_type=MESH
        )

    def send_all(phase, source, dest):
        def one(d, _):
            peer = lax.rem(me + d, blocks)
            pltpu.make_async_remote_copy(
                src_ref=source(peer),
                dst_ref=dest,
                send_sem=send_sem.at[phase],
                recv_sem=recv_sem.at[phase],
                device_id=(peer, member),
                device_id_type=MESH,
            ).start()
            return 0

        lax.fori_loop(1, blocks, one, 0)

    def whom(index):
        turn, kind = split(index, KINDS)
        to = turn + across.astype(F32)
        to = jnp.where(to >= lines, to - lines, to)
        far = 2.0 - 4.0 * split(to, 2)[1]
        step = jnp.where(kind == 1, 1.0, jnp.where(kind == 2, -1.0, far))
        at = jnp.where(kind == 0, 0.0, step) + along.astype(F32)
        at = jnp.where(at < 0, at + LINE, at)
        at = jnp.where(at >= LINE, at - LINE, at)
        return to * LINE + at

    def start(phase, peer, source, dest):
        pltpu.make_async_remote_copy(
            src_ref=source,
            dst_ref=dest,
            send_sem=send_sem.at[phase],
            recv_sem=recv_sem.at[phase],
            device_id=(peer, member),
            device_id_type=MESH,
        ).start()

    def serve(turn, kind):
        to = lax.rem(across + turn, lines)
        at = lax.rem(along + step_to(kind, to) + LINE, LINE)
        return to * LINE + at, serve_s.at[turn * KINDS + kind], serve_r.at[:, my_class]

    def give_back(turn, kind):
        to = lax.rem(across + turn, lines)
        at = lax.rem(along - step_to(kind, across) + LINE, LINE)
        place = lax.rem(lines - turn, lines) * KINDS + kind
        held_class = to * half + lax.rem(at, half)
        return to * LINE + at, term_s.at[:, held_class], term_r.at[place]

    def send_members(phase, source, dest):
        for d in range(1, members):
            pltpu.make_async_remote_copy(
                src_ref=source,
                dst_ref=dest,
                send_sem=send_sem.at[phase],
                recv_sem=recv_sem.at[phase],
                device_id=(me, lax.rem(member + d, members)),
                device_id_type=MESH,
            ).start()

    def bytes_of(phase, ref):
        return pltpu.make_async_remote_copy(
            src_ref=ref,
            dst_ref=ref,
            send_sem=send_sem.at[phase],
            recv_sem=recv_sem.at[phase],
            device_id=(me, member),
            device_id_type=MESH,
        )

    def others(ref):
        return ref.at[pl.ds(0, ref.shape[0] - 1)]

    def scan(q, state):
        count, found = state
        live = (counts[0, q] > 0) & (q != me)
        found = tuple(
            jnp.where(live & (count == k), q, f) for k, f in enumerate(found)
        )
        return count + jnp.where(live, 1, 0), found

    zero = jnp.int32(0)
    _, partners = lax.fori_loop(0, blocks, scan, (zero, (zero,) * PARTNERS))

    target = target_ref[...]
    goal, landing = split(target.astype(F32), rows)
    hits = ones_where(goal == iota((blocks, rows), 0))
    before = ones_where(iota((rows, rows), 0) < iota((rows, rows), 1))
    earlier = dot(hits, before)
    rank = jnp.sum(hits.astype(F32) * earlier, axis=0, keepdims=True)
    high, low = split(landing + 1.0, 16)
    of_rank = ones_where(rank == iota((LANES, rows), 0))
    on_lanes = ((1,), (1,))
    land_high = dot(hits * high.astype(BF), of_rank, on_lanes)
    land_low = dot(hits * low.astype(BF), of_rank, on_lanes)
    lane = lax.broadcasted_iota(jnp.int32, (blocks, LANES), 1)
    listed = jnp.zeros((blocks, LANES), jnp.int32)
    for k in range(PARTNERS):
        listed = jnp.where(lane == LIST_AT + k, partners[k], listed)
    notes = 16.0 * land_high + land_low + listed.astype(F32)
    for p in range(blocks):
        note_s[p] = notes[p : p + 1, :]
    to_slot = ones_where(goal * bucket + rank == iota((loaded, rows), 0))
    put_rows(load_s, dot(to_slot, feat[...]).astype(BF))

    pl.semaphore_wait(barrier, blocks + members - 2)
    send_all(to_notes, lambda p: note_s.at[p], note_r.at[me])
    send_all(0, lambda p: load_s.at[p], load_r.at[me])
    note_r[me] = note_s[me]
    send_members(7, w_ref, w_all.at[member])
    load_r[me] = load_s[me]
    w_all[member] = w_ref[...]
    shift = split(iota(offset.shape, 0), PIECE)[1]
    offset[...] = iota(offset.shape, 1) - shift
    fold = ones_where(iota((LANES, loaded), 0) == split(iota((LANES, loaded), 1), bucket)[1])
    bytes_of(to_notes, others(note_r)).wait_recv()
    for p in range(blocks):
        flat[p : p + 1, :] = note_r[p]
    notes = flat[...]
    high, low = split(notes, 16)
    lands = 16.0 * dot(high.astype(BF), fold) + dot(low.astype(BF), fold)
    unit = split(iota((blocks, loaded), 1), bucket)[0]
    lands = jnp.where(unit == iota((blocks, loaded), 0), lands, 0.0)
    lands = jnp.sum(lands, axis=0, keepdims=True) - 1.0
    regroup = ones_where(lands == iota((rows, loaded), 0))

    bytes_of(0, others(load_r)).wait_recv()
    got = get_rows(load_r)
    regrouped = dot(regroup, got).astype(BF)
    put_rows(spread_s, regrouped)

    def class_of(peer):
        return lax.div(peer, LINE) * half + lax.rem(lax.rem(peer, LINE), half)

    send_all(1, lambda p: spread_s.at[class_of(p)], spread_r.at[me])
    spread_r[me] = spread_s[my_class]

    lists = notes.astype(BF)
    chunk = rows

    def fill_pick_t(i, _):
        first = (i * chunk).astype(F32)
        place = split(iota((chunk, blocks), 0) + first, PARTNERS * PIECE)[0]
        for_whom = ones_where(whom(place) == iota((chunk, blocks), 1))
        nth = split(iota((chunk, LANES), 0) + first, PIECE)[0]
        nth = split(nth, PARTNERS)[1] + LIST_AT
        listed = jnp.where(nth == iota((chunk, LANES), 1), dot(for_whom, lists), 0.0)
        wanted = dot(listed.astype(BF), jnp.full((LANES, held), PIECE, BF))
        match = ones_where(wanted == offset[...])
        pick_t[pl.ds(pl.multiple_of(i * chunk, chunk), chunk), :] = match
        return 0

    lax.fori_loop(0, served // chunk, fill_pick_t, 0)
    bytes_of(1, others(spread_r)).wait_recv()
    turn_rows = KINDS * PARTNERS * PIECE

    def serve_turn(turn, _):
        part = pl.ds(pl.multiple_of(turn * turn_rows, turn_rows), turn_rows)
        pieces = dot(pick_t[part, :], get_rows(spread_r)).astype(BF)
        put_part(serve_s, turn * KINDS, KINDS, pieces)
        for kind in range(KINDS):
            start(2, *serve(turn, kind))
        return 0

    pieces = dot(pick_t[:turn_rows, :], get_rows(spread_r)).astype(BF)
    put_part(serve_s, 0, KINDS, pieces)
    for kind in range(1, KINDS):
        start(2, *serve(0, kind))
    lax.fori_loop(1, lines, serve_turn, 0)
    serve_r[:, my_class] = serve_s[0]

    load_tiles.wait()
    for k in range(meets):
        q = me if k == PARTNERS else partners[k]
        places = [
            jnp.where(s < counts[0, q], tile_row[s, q] * tiles + tile_col[s, q], -1)
            for s in range(slots)
        ]
        for i in range(tiles):
            for j in range(tiles):
                chosen = zero
                live = zero
                for s in range(slots):
                    match = places[s] == i * tiles + j
                    chosen = jnp.where(match, s, chosen)
                    live = jnp.where(match, 1, live)
                values = tv[q, chosen]
                values = values * jnp.full(values.shape, live, jnp.int32).astype(F32).astype(BF)
                adj[pl.ds(i * tile, tile), pl.ds(k * rows + j * tile, tile)] = values
                adj_t[pl.ds(k * rows + j * tile, tile), pl.ds(i * tile, tile)] = values.T

    nth = split(iota((LANES, served), 1), PIECE)[0]
    nth = split(nth, PARTNERS)[1] + LIST_AT
    listed = dot(lists, ones_where(nth == iota((LANES, served), 0)))
    place = split(iota((1, served), 1), PARTNERS * PIECE)[0]
    listed = jnp.where(whom(place) == iota((blocks, served), 0), listed, 0.0)
    wanted = jnp.sum(listed, axis=0, keepdims=True)
    wanted = wanted * PIECE + split(iota((1, served), 1), PIECE)[1]
    part_rows = held // KINDS
    for c in range(KINDS):
        at = iota((part_rows, served), 0) + float(c * part_rows)
        pick[pl.ds(c * part_rows, part_rows), :] = ones_where(wanted == at)

    bytes_of(2, others(serve_s)).wait_recv()
    away = PARTNERS * rows
    share = rows // members
    for c in range(members):
        part = pl.ds(c * share, share)
        mixed = dot(adj[part, :away], get_rows(serve_r)) + dot(adj[part, away:], regrouped)
        mixed_r[member, part] = mixed.astype(BF)
        send_members(8 + c, mixed_r.at[member, part], mixed_r.at[member, part])
    bytes_of(7, others(w_all)).wait_recv()
    some = mixed_r.at[pl.ds(0, members - 1), pl.ds(0, share)]

    bias_part = jnp.zeros((1, wide), F32)
    for c in range(members):
        part = pl.ds(c * share, share)
        bytes_of(8 + c, some).wait_recv()
        pre = dot(mixed_r[0, part], w_all[0])
        for r in range(1, members):
            pre = pre + dot(mixed_r[r, part], w_all[r])
        pre = pre + bias_ref[...]
        sigma = jax.nn.sigmoid(pre)
        outs[c] = (pre * sigma).astype(BF)
        grad = og_ref[part, :].astype(F32) * sigma * (1.0 + pre * (1.0 - sigma))
        grad = grad.astype(BF)
        pg[part, :] = grad
        bias_part = bias_part + jnp.sum(grad.astype(F32), axis=0, keepdims=True)
        mg[part, :] = dot(grad, w_ref[...], on_lanes).astype(BF)
    out_ref[...] = outs[member]

    put_rows(term_s, dot(adj_t[:away], mg[...]).astype(BF))
    for kind in range(1, KINDS):
        start(3, *give_back(0, kind))

    def give_turn(turn, _):
        for kind in range(KINDS):
            start(3, *give_back(turn, kind))
        return 0

    lax.fori_loop(1, lines, give_turn, 0)
    term_r[0] = term_s[:, my_class]
    own[...] = dot(adj_t[away:], mg[...])

    groups = wide // LANES
    for g in range(groups):
        bias_s[g : g + 1, :] = bias_part[:, g * LANES : (g + 1) * LANES]
    for d in range(1, LINE):
        peer = across * LINE + lax.rem(along + d, LINE)
        start(to_notes + 1, peer, bias_s, line_r.at[along])
    line_r[along] = bias_s[...]

    weight_part = dot(mixed_r[member].T, pg[...])
    per_peer = (cols // UNIT) * groups // blocks
    for p in range(blocks):
        for t in range(per_peer):
            band, group = divmod(p * per_peer + t, groups)
            grad_s[p, t] = weight_part[
                band * UNIT : (band + 1) * UNIT, group * LANES : (group + 1) * LANES
            ].astype(BF)
    send_all(5, lambda p: grad_s.at[p], grad_r.at[me])
    grad_r[me] = grad_s[me]

    bytes_of(to_notes + 1, others(line_r)).wait_recv()
    line_s[...] = jnp.sum(line_r[...], axis=0)

    def pass_on(d, _):
        peer = lax.rem(across + d, lines) * LINE + along
        start(to_notes + 2, peer, line_s, plane_r.at[across])
        return 0

    lax.fori_loop(1, lines, pass_on, 0)
    plane_r[across] = line_s[...]

    bytes_of(3, others(term_r)).wait_recv()
    some_lines = max(1, lines // 4)
    together = some_lines * LINE
    for turn in range(lines // some_lines):
        line = lax.rem(lax.div(across, some_lines) * some_lines + turn * some_lines, lines)
        part = pl.ds(pl.multiple_of(line * LINE * PIECE, together * PIECE), together * PIECE)
        sums = dot(pick[part, :], get_rows(term_r)).astype(BF)
        put_part(sum_s, line * LINE, together, sums)

        def hand_back(d, _, line=line):
            peer = line * LINE + lax.rem(me + d, together)
            start(4, peer, sum_s.at[peer], sum_r.at[me])
            return 0

        lax.fori_loop(1 if turn == 0 else 0, together, hand_back, 0)
    sum_r[me] = sum_s[me]

    bytes_of(to_notes + 2, others(plane_r)).wait_recv()
    bg_ref[...] = jnp.sum(plane_r[...], axis=0)

    bytes_of(5, others(grad_r)).wait_recv()
    total = grad_r[0].astype(F32)
    for p in range(1, blocks):
        total = total + grad_r[p].astype(F32)
    total_s[...] = total.astype(BF)
    send_all(6, lambda p: total_s, total_r.at[me])
    total_r[me] = total_s[...]

    bytes_of(6, others(total_r)).wait_recv()
    for p in range(blocks):
        for t in range(per_peer):
            band, group = divmod(p * per_peer + t, groups)
            wg_ref[
                band * UNIT : (band + 1) * UNIT, group * LANES : (group + 1) * LANES
            ] = total_r[p, t].astype(F32)

    bytes_of(4, others(sum_r)).wait_recv()
    stretch = half * PIECE
    for a in range(lines):
        for side in range(2):
            for c in range(half):
                where = pl.ds(a * stretch + c * PIECE, PIECE)
                own[where, :] += sum_r[a * LINE + side * half + c].astype(F32)
    fg_ref[...] = own[...].astype(BF)

    bytes_of(0, others(load_s)).wait_send()
    bytes_of(1, others(spread_r)).wait_send()
    bytes_of(2, others(serve_s)).wait_send()
    bytes_of(3, others(term_r)).wait_send()
    bytes_of(4, others(sum_s)).wait_send()
    bytes_of(5, others(grad_s)).wait_send()
    bytes_of(6, others(total_r)).wait_send()
    bytes_of(7, others(w_all)).wait_send()
    for c in range(members):
        bytes_of(8 + c, some).wait_send()
    bytes_of(to_notes, others(note_r)).wait_send()
    bytes_of(to_notes + 1, others(line_r)).wait_send()
    bytes_of(to_notes + 2, others(plane_r)).wait_send()


def hand_over(*refs):
    for source, dest in zip(refs[: len(refs) // 2], refs[len(refs) // 2 :]):
        dest[...] = source[...]


def per_device(
    features,
    row_target,
    tile_values,
    tile_rows,
    tile_cols,
    tile_counts,
    weight,
    layer_bias,
    out_grad,
):
    blocks = lax.axis_size("blk")
    members = lax.axis_size("rep")
    rows, cols = features.shape
    slots, tile = tile_values.shape[2:4]
    bucket = 2 * rows // blocks
    assert rows == blocks * UNIT and cols == LANES and bucket == PIECE
    wide = weight.shape[1]
    groups = wide // LANES
    pieces = (cols // UNIT) * groups // blocks
    half = blocks // 2
    held = blocks * PIECE
    away = PARTNERS * rows
    meets = PARTNERS + 1
    smem = pl.BlockSpec(memory_space=pltpu.SMEM)
    vmem = pl.BlockSpec(memory_space=pltpu.VMEM)
    results = pl.pallas_call(
        functools.partial(kernel, blocks, members),
        out_shape=(
            jax.ShapeDtypeStruct((rows // members, wide), BF),
            jax.ShapeDtypeStruct((cols, wide), F32),
            jax.ShapeDtypeStruct((groups, LANES), F32),
            jax.ShapeDtypeStruct((rows, cols), BF),
        ),
        in_specs=[
            vmem,
            vmem,
            smem,
            smem,
            smem,
            pl.BlockSpec(memory_space=pl.ANY),
            vmem,
            vmem,
            vmem,
        ],
        out_specs=(vmem,) * 4,
        scratch_shapes=[
            pltpu.VMEM((blocks, slots, tile, tile), BF),
            pltpu.VMEM((blocks, bucket, LANES), BF),
            pltpu.VMEM((blocks, bucket, LANES), BF),
            pltpu.VMEM((half, PIECE, LANES), BF),
            pltpu.VMEM((blocks, PIECE, LANES), BF),
            pltpu.VMEM((away, held), BF),
            pltpu.VMEM((held, away), BF),
            pltpu.VMEM((half, PARTNERS, PIECE, LANES), BF),
            pltpu.VMEM((PARTNERS, half, PIECE, LANES), BF),
            pltpu.VMEM((rows, meets * rows), BF),
            pltpu.VMEM((meets * rows, rows), BF),
            pltpu.VMEM((members, rows, cols), BF),
            pltpu.VMEM((members, cols, wide), BF),
            pltpu.VMEM((rows, wide), BF),
            pltpu.VMEM((members, rows // members, wide), BF),
            pltpu.VMEM((rows, cols), BF),
            pltpu.VMEM((rows, cols), F32),
            pltpu.VMEM((PARTNERS, half, PIECE, LANES), BF),
            pltpu.VMEM((half, PARTNERS, PIECE, LANES), BF),
            pltpu.VMEM((blocks, PIECE, LANES), BF),
            pltpu.VMEM((blocks, PIECE, LANES), BF),
            pltpu.VMEM((blocks, pieces, UNIT, LANES), BF),
            pltpu.VMEM((blocks, pieces, UNIT, LANES), BF),
            pltpu.VMEM((pieces, UNIT, LANES), BF),
            pltpu.VMEM((blocks, pieces, UNIT, LANES), BF),
            pltpu.VMEM((rows, held), F32),
            pltpu.VMEM((blocks, 1, LANES), F32),
            pltpu.VMEM((blocks, 1, LANES), F32),
            pltpu.VMEM((blocks, LANES), F32),
            pltpu.VMEM((groups, LANES), F32),
            pltpu.VMEM((LINE, groups, LANES), F32),
            pltpu.VMEM((groups, LANES), F32),
            pltpu.VMEM((blocks // LINE, groups, LANES), F32),
            pltpu.SemaphoreType.DMA((11 + members,)),
            pltpu.SemaphoreType.DMA((11 + members,)),
            pltpu.SemaphoreType.DMA,
        ],
        compiler_params=pltpu.CompilerParams(
            collective_id=0, has_side_effects=True, vmem_limit_bytes=58 * 2**20
        ),
    )(
        features,
        row_target.reshape(1, rows),
        tile_rows[0].T,
        tile_cols[0].T,
        tile_counts,
        tile_values[0],
        weight,
        layer_bias.reshape(1, wide),
        out_grad,
    )
    output, weight_grad, bias_grad, feature_grad = pl.pallas_call(
        hand_over,
        out_shape=tuple(jax.ShapeDtypeStruct(r.shape, r.dtype) for r in results),
        in_specs=[vmem] * len(results),
        out_specs=(vmem,) * len(results),
    )(*results)
    return output, weight_grad, bias_grad.reshape(wide), feature_grad


def solution(mesh):
    in_specs = (
        P("blk", "rep"),
        P("blk"),
        P("blk", None, None, None, None),
        P("blk", None, None),
        P("blk", None, None),
        P("blk", None),
        P("rep", None),
        P(),
        P("blk", None),
    )
    out_specs = (P(("blk", "rep"), None), P("rep", None), P(), P("blk", "rep"))
    return jax.shard_map(
        per_device, mesh=mesh, in_specs=in_specs, out_specs=out_specs, check_vma=False
    )
```
